128 devices in a mesh: stream: 32 (over y, z, core), span: 4 (over x).
Axes of the slice: x: 4, y: 4, z: 4, core: 2. Of those that a mesh axis runs over, the one named last changes fastest.
Arguments:
- right_side: float32 [256, 4, 64, 512], P('stream', None, None, 'span'), may hold values from -6 to 6
- shift_fine: float32 [256, 64, 512], P('stream', None, 'span'), may hold values from 3 to 9
- diag_blocks: bfloat16 [256, 64, 64, 512], P('stream', None, None, 'span'), may hold values from -0.375 to 0.375
- smoother: bfloat16 [256, 64, 64, 512], P('stream', None, None, 'span'), may hold values from -0.09375 to 0.09375
- couplings: bfloat16 [8, 64, 64], replicated, may hold values from -0.25 to 0.25
- coefficients: float32 [8, 256, 512], P(None, 'stream', 'span'), may hold values from 0.5 to 1.5
- agg_ids: int32 [256, 512], P('stream', 'span'), may hold values from 0 to 31, as said below
- coarse_columns: int32 [32, 4, 32, 5], P('stream', 'span'), may hold values from 0 to 31, as said below
- coarse_blocks: float32 [32, 4, 32, 5, 4096], P('stream', 'span'), may hold values from -0.125 to 0.125
- coarse_shift: float32 [32, 4, 32, 64], P('stream', 'span'), may hold values from 2 to 5
Outputs:
- solution: float32 [256, 4, 64, 512], P('stream', None, None, 'span')
The draws below stay inside these ranges and needn't reach their ends.
Inputs may be any that keep to these rules, and one draw needn't show every extreme that they name: `agg_ids`: within a block of 8 node rows and 128 spanwise nodes, local row s is split into 2 to 4 runs of consecutive spanwise nodes, and the k-th run holds id s * 4 + k; the last local row of every block has 4 runs. `coarse_columns`: index k of a coarse row names an id present in block n_k; at either streamwise end the missing neighbour is replaced by the block itself.
All inputs are finite; a program needn't handle non-finite values.
Results may differ from the reference program's by a relative error of at most 0.004.
Values may be sent and summed in bfloat16 or wider, within the bound.
A program may use at most 256 MiB of HBM per device.

```python
import math
import jax
import jax.numpy as jnp
from jax import lax

VARS = 64
NRHS = 4
S_DEV = 8
SPAN_NODES = 512
AGG_ROW = 4
NNZ = 5
CHEB = 8
SWEEPS = 2
NS = 256
P_DEV = 128
AGG_DEV = 32
N_STREAM = 32
N_SPAN = 4


def aggregate_layout(key):
    base = jax.random.fold_in(key, 4101)
    run_key, cut_key = jax.random.split(base)
    row_total = S_DEV * N_STREAM
    run_counts = jax.random.randint(run_key, (row_total, N_SPAN), 2, AGG_ROW + 1)
    local_rows = jnp.arange(row_total) % S_DEV
    run_counts = jnp.where((local_rows == S_DEV - 1)[:, None], AGG_ROW, run_counts)
    scores = jax.random.randint(cut_key, (row_total, N_SPAN, P_DEV - 1), 0, 1 << 20) * P_DEV + jnp.arange(P_DEV - 1)[None, None, :]
    ignored, chosen = lax.top_k(scores, AGG_ROW - 1)
    cut_points = chosen + 1
    in_use = jnp.arange(AGG_ROW - 1)[None, None, :] < (run_counts - 1)[:, :, None]
    positions = jnp.arange(P_DEV)
    passed = jnp.logical_and(in_use[:, :, :, None], positions[None, None, None, :] >= cut_points[:, :, :, None])
    segment = jnp.sum(passed.astype(jnp.int32), axis=2)
    aggregate_ids = local_rows[:, None, None] * AGG_ROW + segment
    return (aggregate_ids.reshape(row_total, N_SPAN * P_DEV).astype(jnp.int32), run_counts)


def draw_agg_ids(key, part):
    return aggregate_layout(key)[0]


def draw_coarse_columns(key, part):
    ignored, run_counts = aggregate_layout(key)
    block_runs = run_counts.reshape(N_STREAM, S_DEV, N_SPAN).transpose(0, 2, 1)
    pick_key = jax.random.fold_in(key, 4102)
    row_key, slot_key = jax.random.split(pick_key)
    shape_all = (N_STREAM, N_SPAN, AGG_DEV, NNZ)
    stream_step = jnp.array([0, -1, 1, 0, 0], jnp.int32)
    span_step = jnp.array([0, 0, 0, -1, 1], jnp.int32)
    stream_block = jnp.clip(jnp.arange(N_STREAM)[:, None, None, None] + stream_step[None, None, None, :], 0, N_STREAM - 1)
    span_block = (jnp.arange(N_SPAN)[None, :, None, None] + span_step[None, None, None, :]) % N_SPAN
    chosen_rows = jax.random.randint(row_key, shape_all, 0, S_DEV)
    available = block_runs[stream_block, span_block, chosen_rows]
    chosen_slots = jax.random.randint(slot_key, shape_all, 0, available)
    return (chosen_rows * AGG_ROW + chosen_slots).astype(jnp.int32)


def levels(rng, shape, cuts, least, top_value):
    def one(axis_at, blocks):
        heights = jax.random.uniform(jax.random.fold_in(jax.random.fold_in(rng, 6), axis_at), (blocks,), jnp.float32, least / len(cuts), top_value / len(cuts))
        return jnp.repeat(jnp.exp(heights), shape[axis_at] // blocks).reshape((-1,) + (1,) * (len(shape) - axis_at - 1))

    loudness = one(*cuts[0])
    for cut in cuts[1:]:
        loudness = loudness * one(*cut)
    return loudness


def normal_values(rng, shape, scale, limit, cuts=(), dtype=jnp.bfloat16):
    values = jax.random.normal(rng, shape, jnp.float32) * scale
    if len(cuts) > 0:
        values = levels(rng, shape, cuts, -0.22, 0.18) * values
    return jnp.clip(values, min=-limit, max=limit).astype(dtype)


def setup_inputs(seed: int = 0) -> dict:
    key_list = jax.random.split(jax.random.key(seed), 11)
    return {
        "right_side": normal_values(key_list[0], (NS, NRHS, VARS, SPAN_NODES), 1.0, 6.0, ((0, 32), (3, 4)), jnp.float32),
        "shift_fine": jnp.clip(jnp.exp(math.log(9.0) - 1.0986123 * jax.random.uniform(key_list[1], (NS, VARS, SPAN_NODES), jnp.float32) ** levels(key_list[1], (NS, VARS, SPAN_NODES), ((0, 32), (2, 4)), -0.2, 0.2)), 3.0, 9.0),
        "diag_blocks": normal_values(key_list[2], (NS, VARS, VARS, SPAN_NODES), 0.06, 0.375, ((0, 32), (3, 4))),
        "smoother": normal_values(key_list[3], (NS, VARS, VARS, SPAN_NODES), 0.015, 0.09375, ((0, 32), (3, 4))),
        "couplings": normal_values(key_list[4], (8, VARS, VARS), (8 * VARS) ** -0.5, 0.25),
        "coefficients": jnp.clip(0.5 + 1.0 * jax.random.uniform(key_list[5], (8, NS, SPAN_NODES), jnp.float32) ** levels(key_list[5], (8, NS, SPAN_NODES), ((1, 32), (2, 4)), -0.2, 0.2), 0.5, 1.5),
        "agg_ids": draw_agg_ids(jax.random.fold_in(key_list[10], 71), 0),
        "coarse_columns": draw_coarse_columns(jax.random.fold_in(key_list[10], 71), 0),
        "coarse_blocks": normal_values(key_list[8], (N_STREAM, N_SPAN, AGG_DEV, NNZ, VARS * VARS), (0.4 / (NNZ * VARS) ** 0.5), 0.125, ((0, 32), (1, 4)), jnp.float32),
        "coarse_shift": jnp.clip(jnp.exp(math.log(5.0) - 0.916290732 * jax.random.uniform(key_list[9], (N_STREAM, N_SPAN, AGG_DEV, VARS), jnp.float32) ** levels(key_list[9], (N_STREAM, N_SPAN, AGG_DEV, VARS), ((0, 32), (1, 4)), -0.2, 0.2)), 2.0, 5.0),
    }


OMEGA = 0.3
OFFSETS = ((-2, 0), (-1, 0), (1, 0), (2, 0), (0, -2), (0, -1), (0, 1), (0, 2))
PRECISE = lax.Precision.HIGHEST

def speed_of(positions, extent):
    return jnp.sqrt(1.0 + 8.0 * (positions.astype(jnp.float32) + 0.5) / extent)

def batched_blocks(blocks, operand):

    def per_row(operands):
        return jnp.einsum('abp,vbp->vap', operands[0].astype(jnp.float32), operands[1].astype(jnp.float32))
    return lax.map(per_row, (blocks, operand))

def apply_fine(vector_field, shift_fine, diag_blocks, couplings, coefficients, node_speed):
    rounded = vector_field.astype(jnp.bfloat16)
    padded = jnp.pad(rounded, ((2, 2), (0, 0), (0, 0), (0, 0)))
    padded = jnp.concatenate([padded[:, :, :, -2:], padded, padded[:, :, :, :2]], axis=3)
    stream_count = rounded.shape[0]
    span_count = rounded.shape[3]
    result = shift_fine[:, None, :, :] * rounded.astype(jnp.float32) + batched_blocks(diag_blocks, rounded)
    coupled = jnp.zeros(result.shape, jnp.float32)
    for number in range(8):
        step_stream, step_span = OFFSETS[number]
        shifted = padded[2 + step_stream:2 + step_stream + stream_count, :, :, 2 + step_span:2 + step_span + span_count]
        product_term = jnp.einsum('ab,svbp->svap', couplings[number].astype(jnp.float32), shifted.astype(jnp.float32))
        coupled = coupled + coefficients[number][:, None, None, :] * product_term
    return result + node_speed[:, None, None, None] * coupled

def smooth(residual, shift_fine, smoother):
    return residual / shift_fine[:, None, :, :] + batched_blocks(smoother, residual.astype(jnp.bfloat16))

def coarse_apply(vector_field, columns, blocks, coarse_shift, live_slots, coarse_speed):
    padded = jnp.pad(vector_field, ((1, 1), (0, 0), (0, 0), (0, 0)))
    padded = jnp.concatenate([padded[:, -1:], padded, padded[:, :1]], axis=1)
    neighbors = (padded[1:-1, 1:-1], padded[:-2, 1:-1], padded[2:, 1:-1], padded[1:-1, :-2], padded[1:-1, 2:])
    row_shape = vector_field.shape[:3] + (NRHS, VARS)
    coupled = jnp.zeros(row_shape, jnp.float32)
    for number in range(NNZ):
        index_table = jnp.broadcast_to(columns[:, :, :, number][:, :, :, None], vector_field.shape).astype(jnp.int32)
        picked = jnp.take_along_axis(neighbors[number], index_table, axis=2).reshape(row_shape)
        coupled = coupled + jnp.einsum('pqgab,pqgvb->pqgva', blocks[:, :, :, number], picked, precision=PRECISE)
    result = coarse_shift[:, :, :, None, :] * vector_field.reshape(row_shape) + coarse_speed[:, None, None, None, None] * coupled
    return (live_slots[:, :, :, None, None] * result).reshape(vector_field.shape)

def chebyshev(matvec, coarse_rhs, upper_bound):
    upper_edge = 1.05 * upper_bound
    lower_edge = upper_edge / 20.0
    middle = 0.5 * (upper_edge + lower_edge)
    spread = 0.5 * (upper_edge - lower_edge)
    ratio_sigma = middle / spread
    rho_now = 1.0 / ratio_sigma
    iterate = jnp.zeros_like(coarse_rhs)
    remainder = coarse_rhs
    direction = coarse_rhs / middle
    for number in range(CHEB):
        iterate = iterate + direction
        if number + 1 < CHEB:
            remainder = remainder - matvec(direction)
            rho_next = 1.0 / (2.0 * ratio_sigma - rho_now)
            direction = rho_next * rho_now * direction + 2.0 * rho_next / spread * remainder
            rho_now = rho_next
    return iterate

def reference(right_side, shift_fine, diag_blocks, smoother, couplings, coefficients, agg_ids, coarse_columns, coarse_blocks, coarse_shift):
    node_speed = speed_of(jnp.arange(NS), NS)

    def apply_field(vector_field):
        return apply_fine(vector_field, shift_fine, diag_blocks, couplings, coefficients, node_speed)
    solution = jnp.zeros(right_side.shape, jnp.float32)
    for repeat in range(SWEEPS):
        if repeat == 0:
            residual = right_side
        else:
            residual = right_side - apply_field(solution)
        solution = solution + OMEGA * smooth(residual, shift_fine, smoother)
    residual = right_side - apply_field(solution)
    grouped_ids = agg_ids.reshape(N_STREAM, S_DEV, N_SPAN, P_DEV)
    members = (grouped_ids[:, :, :, :, None] == jnp.arange(AGG_DEV)[None, None, None, None, :]).astype(jnp.float32)
    grouped = residual.reshape(N_STREAM, S_DEV, NRHS, VARS, N_SPAN, P_DEV)
    coarse_rhs = jnp.einsum('psqjg,psvaqj->pqgva', members, grouped, precision=PRECISE).reshape(N_STREAM, N_SPAN, AGG_DEV, NRHS * VARS)
    live_slots = (lax.optimization_barrier(jnp.sum(members, axis=(1, 3))) > 0.0).astype(jnp.float32)
    blocks = coarse_blocks.reshape(N_STREAM, N_SPAN, AGG_DEV, NNZ, VARS, VARS)
    coarse_speed = speed_of(jnp.arange(N_STREAM), N_STREAM)
    absolute = lax.optimization_barrier(jnp.sum(jnp.abs(blocks), axis=(3, 5)))
    upper_bound = jnp.max(live_slots[:, :, :, None] * (coarse_shift + coarse_speed[:, None, None, None] * absolute))

    def matvec(direction):
        return coarse_apply(direction, coarse_columns, blocks, coarse_shift, live_slots, coarse_speed)
    coarse_solution = chebyshev(matvec, coarse_rhs, upper_bound)
    prolonged = jnp.einsum('psqjg,pqgz->pszqj', members, coarse_solution, precision=PRECISE).reshape(NS, NRHS, VARS, SPAN_NODES)
    image_field = apply_field(prolonged)
    solution = solution + prolonged - OMEGA * smooth(image_field, shift_fine, smoother)
    for repeat in range(SWEEPS):
        residual = right_side - apply_field(solution)
        solution = solution + OMEGA * smooth(residual, shift_fine, smoother)
    return solution
```

```python
import functools

import jax
import jax.numpy as jnp
from jax import lax
from jax.experimental import pallas as pl
from jax.experimental.pallas import tpu as pltpu
from jax.sharding import PartitionSpec as P

OMEGA = 0.3
CHEB = 8
BF = jnp.bfloat16
F32 = jnp.float32
MESH = pl.DeviceIdType.MESH
NT = (((1,), (1,)), ((), ()))
PAIRS = 4
ROWS = 512
EDGE = 16
WROWS = ROWS + 2 * EDGE
UNROLL = 16


def iota(shape, dim):
    return lax.broadcasted_iota(jnp.int32, shape, dim)


def one_zero(mask):
    return jnp.where(mask, 1.0, 0.0).astype(BF)


def dot(left, right):
    return jnp.dot(left, right, preferred_element_type=F32)


def dot_nt(left, right):
    return lax.dot_general(left, right, NT, preferred_element_type=F32)


def hi_lo(value):
    high = value.astype(BF)
    return high, (value - high.astype(F32)).astype(BF)


def block_tile(blocks, low, quad, step):
    left_half = iota((16, 128), 1) < 64
    none = jnp.zeros((16, 128), BF)
    first, second = low
    operand = jnp.concatenate(
        [
            jnp.concatenate([jnp.where(left_half, first, none), none], 1),
            jnp.concatenate([jnp.where(left_half, none, first), none], 1),
            jnp.concatenate([none, jnp.where(left_half, second, none)], 1),
            jnp.concatenate([none, jnp.where(left_half, none, second)], 1),
        ],
        0,
    )
    rows = pl.ds(pl.multiple_of(step * 256, 256), 256)
    weights = jnp.concatenate([blocks[2 * quad, rows, :], blocks[2 * quad + 1, rows, :]], 1)
    product = dot_nt(operand, weights)
    top = iota((8, 128), 0) < 4
    left = iota((8, 128), 1) < 64
    results = []
    for half in range(2):
        pieces = []
        for part in range(2):
            even = product[32 * half + 8 * part : 32 * half + 8 * part + 8, 128 * part : 128 * part + 128]
            odd = product[32 * half + 16 + 8 * part : 32 * half + 24 + 8 * part, 128 * part : 128 * part + 128]
            kept = jnp.where(top, even, odd)
            moved = pltpu.roll(jnp.where(top, odd, even), 64, 1)
            pieces.append(jnp.where(top == left, kept, moved))
        results.append(jnp.concatenate(pieces, 0))
    return results


def relayout(raw, blocks, pair):
    def some_rows(group, carry):
        turned = []
        for number in range(16):
            row = group * 16 + number
            source = jnp.concatenate([raw[2 * pair, row], raw[2 * pair + 1, row]], 0)
            turned.append(source.T)
        for part in range(8):
            cube = jnp.stack([one[16 * part : 16 * part + 16] for one in turned], 0)
            cube = jnp.transpose(cube, (1, 0, 2))
            for node in range(16):
                place = pl.multiple_of((part * 16 + node) * 64 + group * 16, 16)
                blocks[pair, pl.ds(place, 16), :] = cube[node]
        return carry

    lax.fori_loop(0, 4, some_rows, 0)


def kernel(
    stream_total,
    span_total,
    rhs_hbm, shift_hbm, diag_hbm, smooth_hbm, couple_hbm, coef_hbm, ids_hbm, cols_hbm, coarse_hbm, cshift_hbm,
    out_hbm,
    raw_rhs, raw_shift, raw_diag, raw_smooth, raw_couple, raw_coef, raw_ids, raw_cols, raw_coarse, raw_cshift,
    diag, smoother, rhs, shift, inverse, field, image, residual, low, wide, coef, couple,
    member, member_t, spread, pick, live, cshift, z_now, t_now, d_now, coarse_own, coarse_got, picked,
    bound, bound_got, idpad,
    load_sem, halo_send, halo_recv, coarse_send, coarse_recv, bound_send, bound_recv, store_sem,
):
    position = lax.axis_index("stream")
    across = lax.axis_index("span")
    after = lax.rem(position + 1, stream_total)
    before = lax.rem(position + stream_total - 1, stream_total)
    right = lax.rem(across + 1, span_total)
    left = lax.rem(across + span_total - 1, span_total)
    group = min(8, stream_total)
    groups = stream_total // group

    stages = [[], [], []]
    for step in range(1, span_total):
        stages[0].append((position, lax.rem(across + step, span_total)))
    base = (position // group) * group
    for step in range(1, group):
        stages[1].append((base + lax.rem(position - base + step, group), across))
    for step in range(1, groups):
        stages[2].append((lax.rem(position + step * group, stream_total), across))
    partners = [who for stage in stages for who in stage]
    greeted = partners + [(after, across), (before, across)]

    barrier = pltpu.get_barrier_semaphore()
    for who in greeted:
        pl.semaphore_signal(barrier, inc=1, device_id=who, device_id_type=MESH)

    loads = []

    def load(source, target):
        copy = pltpu.make_async_copy(source, target, load_sem.at[len(loads)])
        copy.start()
        loads.append(copy)
        return copy

    load_rhs = load(rhs_hbm, raw_rhs)
    load_shift = load(shift_hbm, raw_shift)
    load_ids = load(ids_hbm, raw_ids)
    load_cols = load(cols_hbm, raw_cols)
    load_cshift = load(cshift_hbm, raw_cshift)
    load_couple = load(couple_hbm, raw_couple)
    load_coef = load(coef_hbm, raw_coef)
    load_smooth = [
        load(smooth_hbm.at[pl.ds(2 * pair, 2)], raw_smooth.at[pl.ds(2 * pair, 2)]) for pair in range(PAIRS)
    ]
    load_coarse = load(coarse_hbm, raw_coarse)
    load_diag = [load(diag_hbm.at[pl.ds(2 * pair, 2)], raw_diag.at[pl.ds(2 * pair, 2)]) for pair in range(PAIRS)]

    def speed_of(place, extent):
        return jnp.sqrt(1.0 + 8.0 * (place + 0.5) / extent)

    here = position.astype(F32)
    coarse_speed = speed_of(jnp.full((1, 128), here, F32), float(stream_total))

    def spread_part(number, carry):
        rows = iota((128, 128), 0)
        lanes = iota((128, 128), 1)
        want = 2 * number + lax.shift_right_logical(rows, 6)
        spread[pl.ds(pl.multiple_of(number * 128, 128), 128), :] = one_zero((lanes & 63) == want)
        return carry

    lax.fori_loop(0, 32, spread_part, 0)

    load_rhs.wait()
    for pair in range(PAIRS):
        for vector in range(4):
            block = jnp.concatenate([raw_rhs[2 * pair, vector], raw_rhs[2 * pair + 1, vector]], 0)
            rhs[pair, pl.ds(vector, 128, stride=4), :] = block.T
    load_shift.wait()
    for pair in range(PAIRS):
        block = jnp.concatenate([raw_shift[2 * pair], raw_shift[2 * pair + 1]], 0).T
        for vector in range(4):
            shift[pair, pl.ds(vector, 128, stride=4), :] = block
        block = 1.0 / block
        for vector in range(4):
            inverse[pair, pl.ds(vector, 128, stride=4), :] = block

    load_ids.wait()
    idpad[...] = jnp.zeros(idpad.shape, BF)
    ids16 = jnp.concatenate([raw_ids[...].astype(F32), jnp.zeros((8, 128), F32)], 0).astype(BF)
    idpad[0:16, :] = ids16
    rows = iota((128, 128), 0)
    lanes = iota((128, 128), 1)
    expand = one_zero(lanes == lax.shift_right_logical(rows & 31, 2))
    by_slot = dot(expand, idpad[...])
    slot = (rows & 31).astype(F32)
    found = jnp.max(jnp.where(by_slot == slot, 1.0, 0.0), axis=1, keepdims=True)
    live[...] = jnp.broadcast_to(found, (128, 128))
    by_slot = by_slot.astype(BF)
    rows = iota((128, 512), 0)
    lanes = iota((128, 512), 1)
    node_of = one_zero(lax.shift_right_logical(lanes, 2) == rows)
    wide_ids = dot(by_slot, node_of)
    same = (lanes & 3) == lax.shift_right_logical(rows, 5)
    member[...] = one_zero(jnp.logical_and(wide_ids == (rows & 31).astype(F32), same))
    rows = iota((512, 128), 0)
    lanes = iota((512, 128), 1)
    of_node = one_zero(lax.shift_right_logical(rows, 2) == lanes)
    tall_ids = dot_nt(of_node, by_slot)
    same = (rows & 3) == lax.shift_right_logical(lanes, 5)
    member_t[...] = one_zero(jnp.logical_and(tall_ids == (lanes & 31).astype(F32), same))

    load_cols.wait()
    rows = iota((128, 32), 0)
    lanes = iota((128, 32), 1)
    repeat_rows = (rows & 31) == lanes
    rows = iota((128, 128), 0)
    lanes = iota((128, 128), 1)
    same = lax.shift_right_logical(rows, 5) == lax.shift_right_logical(lanes, 5)
    for number in range(5):
        line = jnp.broadcast_to(raw_cols[number : number + 1, :].astype(F32), (128, 32)).astype(BF)
        column = dot_nt(one_zero(repeat_rows), line)
        chosen = jnp.logical_and(column == (lanes & 31).astype(F32), same)
        if number == 1:
            chosen = jnp.logical_and(chosen, position > 0)
        if number == 2:
            chosen = jnp.logical_and(chosen, position < stream_total - 1)
        pick[number] = one_zero(chosen)

    load_cshift.wait()
    twice = jnp.where((iota((64, 128), 1) & 63) == iota((64, 128), 0), 1.0, 0.0)
    doubled = jnp.dot(raw_cshift[...], twice, precision=lax.Precision.HIGHEST, preferred_element_type=F32)
    for vector in range(4):
        cshift[32 * vector : 32 * vector + 32, :] = doubled

    load_couple.wait()
    for number in range(8):
        one = raw_couple[number].astype(F32)
        none = jnp.zeros((64, 64), F32)
        both = jnp.concatenate([jnp.concatenate([one, none], 1), jnp.concatenate([none, one], 1)], 0)
        couple[number * 128 : number * 128 + 128, :] = both.T.astype(BF)

    load_coef.wait()
    rows = iota((512, 128), 0)
    lanes = iota((512, 128), 1)
    of_node = one_zero(lax.shift_right_logical(rows, 2) == lanes)
    place = iota((8, 128), 0)
    node_speed = speed_of(here * 8.0 + place.astype(F32), float(stream_total * 8))
    first = position == 0
    last = position == stream_total - 1
    for number in range(8):
        weights = node_speed * raw_coef[number]
        if number == 0:
            weights = jnp.where(jnp.logical_and(first, place < 2), 0.0, weights)
        if number == 1:
            weights = jnp.where(jnp.logical_and(first, place < 1), 0.0, weights)
        if number == 2:
            weights = jnp.where(jnp.logical_and(last, place > 6), 0.0, weights)
        if number == 3:
            weights = jnp.where(jnp.logical_and(last, place > 5), 0.0, weights)
        for half in range(2):
            lines = jnp.concatenate(
                [jnp.broadcast_to(weights[4 * half + i : 4 * half + i + 1, :], (64, 128)) for i in range(4)], 0
            ).astype(BF)
            laid = dot_nt(of_node, lines).astype(BF)
            coef[number, 2 * half] = laid[:, :128]
            coef[number, 2 * half + 1] = laid[:, 128:]

    pl.semaphore_wait(barrier, len(greeted))

    bound_copies = [
        pltpu.make_async_remote_copy(
            src_ref=bound.at[stage],
            dst_ref=bound_got.at[slot_number],
            send_sem=bound_send.at[slot_number],
            recv_sem=bound_recv.at[slot_number],
            device_id=who,
            device_id_type=MESH,
        )
        for slot_number, (stage, who) in enumerate(
            [(stage, who) for stage in range(3) for who in stages[stage]]
        )
    ]
    starts = [0, len(stages[0]), len(stages[0]) + len(stages[1]), len(partners)]

    def bound_begin(stage):
        for number in range(starts[stage], starts[stage + 1]):
            bound_copies[number].start()

    def bound_end(stage):
        value = bound[stage]
        for number in range(starts[stage], starts[stage + 1]):
            bound_copies[number].wait()
            value = jnp.maximum(value, bound_got[number])
        bound[stage + 1] = value

    def coarse_bound():
        load_coarse.wait()
        total = jnp.zeros((64, 128), F32)
        for number in range(32):
            columns = slice(128 * number, 128 * number + 128)
            size = jnp.abs(raw_coarse[0, :, columns])
            for kind in range(1, 5):
                size = size + jnp.abs(raw_coarse[kind, :, columns])
            high, rest = hi_lo(size)
            total = total + dot(jnp.concatenate([high, rest], 0), spread[columns, :])
        largest = live[0:32, :] * (cshift[0:32, :] + coarse_speed * (total[0:32] + total[32:64]))
        bound[0] = jnp.broadcast_to(jnp.max(jnp.max(largest, axis=1, keepdims=True), axis=0, keepdims=True), (8, 128))

    def halo_copies(parity):
        def copy(number, source, target, who):
            return pltpu.make_async_remote_copy(
                src_ref=source,
                dst_ref=target,
                send_sem=halo_send.at[parity, number],
                recv_sem=halo_recv.at[parity, number],
                device_id=who,
                device_id_type=MESH,
            )

        mine = pl.ds(EDGE, ROWS)
        inner = pl.ds(1, PAIRS)
        return [
            copy(0, wide.at[parity, PAIRS, mine], wide.at[parity, 0, mine], (after, across)),
            copy(1, wide.at[parity, 1, mine], wide.at[parity, PAIRS + 1, mine], (before, across)),
            copy(2, wide.at[parity, inner, pl.ds(ROWS, EDGE)], wide.at[parity, inner, pl.ds(0, EDGE)], (position, right)),
            copy(3, wide.at[parity, inner, pl.ds(EDGE, EDGE)], wide.at[parity, inner, pl.ds(ROWS + EDGE, EDGE)], (position, left)),
        ]

    def smooth_step(parity):
        following = 1 - parity

        def tiles(number, carry):
            for inside in range(UNROLL):
                tile = number * UNROLL + inside
                quad, step = tile // 32, lax.rem(tile, 32)
                rows = pl.ds(pl.multiple_of(step * 16, 16), 16)
                shifted = pl.ds(pl.multiple_of(step * 16 + EDGE, 16), 16)
                operand = [low[2 * quad + half, rows, :] for half in range(2)]
                parts = block_tile(smoother, operand, quad, step)
                for half in range(2):
                    pair = 2 * quad + half
                    change = residual[pair, rows, :] * inverse[pair, rows, :] + parts[half]
                    value = field[pair, rows, :] + OMEGA * change
                    field[pair, rows, :] = value
                    wide[following, pair + 1, shifted, :] = value.astype(BF)
            return carry

        lax.fori_loop(0, 64 // UNROLL, tiles, 0)

    def operator_inner(parity):
        def tiles(number, carry):
            for inside in range(UNROLL):
                tile = number * UNROLL + inside
                quad, step = tile // 32, lax.rem(tile, 32)
                rows = pl.ds(pl.multiple_of(step * 16, 16), 16)
                shifted = pl.ds(pl.multiple_of(step * 16 + EDGE, 16), 16)
                operand = [wide[parity, 2 * quad + half + 1, shifted, :] for half in range(2)]
                parts = block_tile(diag, operand, quad, step)
                for half in range(2):
                    pair = 2 * quad + half
                    image[pair, rows, :] = shift[pair, rows, :] * operand[half].astype(F32) + parts[half]
            return carry

        lax.fori_loop(0, 64 // UNROLL, tiles, 0)

    def operator_outer(parity, scale):
        left_half = iota((128, 128), 1) < 64

        def chunks(number, carry):
            pair, start = number // 4, lax.rem(number, 4) * 128
            rows = pl.ds(pl.multiple_of(start, 128), 128)

            def at(which):
                return wide[parity, which, pl.ds(pl.multiple_of(start + EDGE, 16), 128), :]

            here_now, lower, upper = at(pair + 1), at(pair), at(pair + 2)
            around = wide[parity, pair + 1, pl.ds(pl.multiple_of(start, 16), 128 + 2 * EDGE), :]
            shifted = [
                lower,
                pltpu.roll(jnp.where(left_half, here_now, lower).astype(F32), 64, 1).astype(BF),
                pltpu.roll(jnp.where(left_half, upper, here_now).astype(F32), 64, 1).astype(BF),
                upper,
                around[EDGE - 8 : EDGE + 120],
                around[EDGE - 4 : EDGE + 124],
                around[EDGE + 4 : EDGE + 132],
                around[EDGE + 8 : EDGE + 136],
            ]
            operand = jnp.concatenate([coef[m, pair, rows, :] * shifted[m] for m in range(8)], 1)
            value = scale * rhs[pair, rows, :] - (image[pair, rows, :] + dot(operand, couple[...]))
            residual[pair, rows, :] = value
            low[pair, rows, :] = value.astype(BF)
            return carry

        lax.fori_loop(0, 16, chunks, 0)

    def coarse_copies(parity):
        targets = [(after, across), (before, across), (position, right), (position, left)]
        return [
            pltpu.make_async_remote_copy(
                src_ref=coarse_own.at[parity],
                dst_ref=coarse_got.at[parity, number],
                send_sem=coarse_send.at[parity, number],
                recv_sem=coarse_recv.at[parity, number],
                device_id=who,
                device_id_type=MESH,
            )
            for number, who in enumerate(targets)
        ]

    def restrict():
        total = jnp.zeros((128, 512), F32)
        parts = []
        for pair in range(PAIRS):
            high, rest = hi_lo(residual[pair])
            parts.append(dot(member[...], high) + dot(member[...], rest))
        left_half = iota((8, 128), 1) < 64
        top = iota((8, 128), 0) < 4
        for vector in range(4):
            for pair in range(PAIRS):
                begin = 32 * vector + 8 * pair
                own = jnp.where(top == left_half, parts[pair][begin : begin + 8, :], 0.0)
                t_now[begin : begin + 8, :] = own + pltpu.roll(own, 64, 1)

    def coarse_product(got):
        for number in range(5):
            value = dot(pick[number], got[number])
            picked[number] = value + pltpu.roll(value, 64, 1)
        total = jnp.zeros((128, 128), F32)
        for column in range(16):
            sides = []
            for side in range(2):
                begin = 256 * column + 128 * side
                blocks = [raw_coarse[k, :, begin : begin + 128] for k in range(5)]
                pieces = []
                for vector in range(4):
                    part = blocks[0] * picked[0, 32 * vector : 32 * vector + 32, :]
                    for k in range(1, 5):
                        part = part + blocks[k] * picked[k, 32 * vector : 32 * vector + 32, :]
                    pieces.append(part.astype(BF))
                sides.append(jnp.concatenate(pieces, 0))
            operand = jnp.concatenate(sides, 1)
            total = total + dot(operand, spread[256 * column : 256 * column + 256, :])
        return total

    def coarse_solve():
        upper_edge = 1.05 * bound[3]
        lower_edge = upper_edge / 20.0
        middle = 0.5 * (upper_edge + lower_edge)
        gap = 0.5 * (upper_edge - lower_edge)
        sigma = middle / gap
        restrict()
        d_now[...] = t_now[...] / middle[0:1, :]
        z_now[...] = jnp.zeros((128, 128), F32)
        left_half = iota((128, 128), 1) < 64

        def step(number, rho):
            parity = lax.rem(number, 2)
            direction = d_now[...]
            high, rest = hi_lo(direction)
            coarse_own[parity] = jnp.where(left_half, high, rest)
            copies = coarse_copies(parity)
            for copy in copies:
                copy.start()
            z_now[...] = z_now[...] + direction
            for copy in copies:
                copy.wait()
            got = [coarse_own[parity]] + [coarse_got[parity, k] for k in range(4)]
            coupled = coarse_product(got)
            t_next = t_now[...] - live[...] * (cshift[...] * direction + coarse_speed * coupled)
            t_now[...] = t_next
            rho_next = 1.0 / (2.0 * sigma - rho)
            d_now[...] = (rho_next * rho)[0:1, :] * direction + (2.0 * rho_next / gap)[0:1, :] * t_next
            return rho_next

        lax.fori_loop(0, CHEB - 1, step, 1.0 / sigma)
        z_now[...] = z_now[...] + d_now[...]

    def prolong(parity):
        following = 1 - parity
        slots = lax.shift_right_logical(iota((128, 128), 0) & 31, 2)
        half = lax.shift_right_logical(iota((128, 128), 1), 6)
        twice = jnp.concatenate([member_t[...], member_t[...]], 1)
        for pair in range(PAIRS):
            high, rest = hi_lo(jnp.where(slots == 2 * pair + half, z_now[...], 0.0))
            value = dot(twice, jnp.concatenate([high, rest], 0))
            field[pair] = field[pair] + value
            wide[following, pair + 1, EDGE : EDGE + ROWS, :] = value.astype(BF)

    field[...] = jnp.zeros(field.shape, F32)
    for pair in range(PAIRS):
        residual[pair] = rhs[pair]
        low[pair] = rhs[pair].astype(BF)

    def round_of(number, carry):
        parity = lax.rem(number, 2)

        @pl.when(number == 0)
        def _():
            for pair in range(PAIRS):
                load_smooth[pair].wait()
                relayout(raw_smooth, smoother, pair)
            coarse_bound()
            bound_begin(0)

        @pl.when(number > 0)
        def _():
            operator_inner(parity)
            copies = halo_copies(parity)
            for copy in copies:
                copy.wait()
            scale = jnp.where(number == 3, 0.0, 1.0)
            operator_outer(parity, scale)

        @pl.when(number == 2)
        def _():
            bound_end(2)
            coarse_solve()
            prolong(parity)

        @pl.when(number != 2)
        def _():
            smooth_step(parity)

        @pl.when(number < 5)
        def _():
            for copy in halo_copies(1 - parity):
                copy.start()

        @pl.when(number == 0)
        def _():
            bound_end(0)
            bound_begin(1)
            for pair in range(PAIRS):
                load_diag[pair].wait()
                relayout(raw_diag, diag, pair)

        @pl.when(number == 1)
        def _():
            bound_end(1)
            bound_begin(2)

        return carry

    lax.fori_loop(0, 6, round_of, 0)

    stores = []
    for pair in range(PAIRS):
        for vector in range(4):
            block = field[pair, pl.ds(vector, 128, stride=4), :].T
            raw_rhs[2 * pair, vector] = block[0:64]
            raw_rhs[2 * pair + 1, vector] = block[64:128]
        copy = pltpu.make_async_copy(
            raw_rhs.at[pl.ds(2 * pair, 2)], out_hbm.at[pl.ds(2 * pair, 2)], store_sem.at[pair]
        )
        copy.start()
        stores.append(copy)
    for copy in stores:
        copy.wait()


def local(stream_total, span_total, right_side, shift_fine, diag_blocks, smoother, couplings, coefficients,
          agg_ids, coarse_columns, coarse_blocks, coarse_shift):
    columns = jnp.transpose(coarse_columns[0, 0], (1, 0))
    blocks = jnp.transpose(coarse_blocks[0, 0], (1, 0, 2))
    vm = pltpu.VMEM
    dma = pltpu.SemaphoreType.DMA
    partners = (span_total - 1) + (min(8, stream_total) - 1) + (stream_total // min(8, stream_total) - 1)
    shape = (PAIRS, ROWS, 128)
    scratch = [
        vm((8, 4, 64, 128), F32), vm((8, 64, 128), F32), vm((8, 64, 64, 128), BF), vm((8, 64, 64, 128), BF),
        vm((8, 64, 64), BF), vm((8, 8, 128), F32), vm((8, 128), jnp.int32), vm((5, 32), jnp.int32),
        vm((5, 32, 4096), F32), vm((32, 64), F32),
        vm((PAIRS, 8192, 128), BF), vm((PAIRS, 8192, 128), BF), vm(shape, F32), vm(shape, F32), vm(shape, F32),
        vm(shape, F32), vm(shape, F32), vm(shape, F32), vm(shape, BF), vm((2, PAIRS + 2, WROWS, 128), BF),
        vm((8,) + shape, BF), vm((1024, 128), BF),
        vm((128, 512), BF), vm((512, 128), BF), vm((4096, 128), BF), vm((5, 128, 128), BF), vm((128, 128), F32),
        vm((128, 128), F32), vm((128, 128), F32), vm((128, 128), F32), vm((128, 128), F32),
        vm((2, 128, 128), BF), vm((2, 4, 128, 128), BF), vm((5, 128, 128), F32),
        vm((4, 8, 128), F32), vm((partners, 8, 128), F32), vm((128, 128), BF),
        dma((16,)), dma((2, 4)), dma((2, 4)), dma((2, 4)), dma((2, 4)), dma((partners,)), dma((partners,)), dma((4,)),
    ]
    anywhere = pl.BlockSpec(memory_space=pl.ANY)
    return pl.pallas_call(
        functools.partial(kernel, stream_total, span_total),
        out_shape=jax.ShapeDtypeStruct(right_side.shape, F32),
        in_specs=[anywhere] * 10,
        out_specs=anywhere,
        scratch_shapes=scratch,
        compiler_params=pltpu.CompilerParams(
            collective_id=0, has_side_effects=True, vmem_limit_bytes=60 * 1024 * 1024
        ),
        name="cycle",
    )(right_side, shift_fine, diag_blocks, smoother, couplings, coefficients, agg_ids, columns, blocks,
      coarse_shift[0, 0])


def solution(mesh):
    return jax.shard_map(
        functools.partial(local, mesh.shape["stream"], mesh.shape["span"]),
        mesh=mesh,
        in_specs=(
            P("stream", None, None, "span"),
            P("stream", None, "span"),
            P("stream", None, None, "span"),
            P("stream", None, None, "span"),
            P(),
            P(None, "stream", "span"),
            P("stream", "span"),
            P("stream", "span", None, None),
            P("stream", "span", None, None, None),
            P("stream", "span", None, None),
        ),
        out_specs=P("stream", None, None, "span"),
        check_vma=False,
    )
```

```python
import functools

import jax
import jax.numpy as jnp
from jax import lax
from jax.experimental import pallas as pl
from jax.experimental.pallas import tpu as pltpu
from jax.sharding import PartitionSpec as P

OMEGA = 0.3
CHEB = 8
BF = jnp.bfloat16
F32 = jnp.float32
MESH = pl.DeviceIdType.MESH
NT = (((1,), (1,)), ((), ()))
PAIRS = 4
ROWS = 512
EDGE = 16
WROWS = ROWS + 2 * EDGE


def iota(shape, dim):
    return lax.broadcasted_iota(jnp.int32, shape, dim)


def one_zero(mask):
    return jnp.where(mask, 1.0, 0.0).astype(BF)


def dot(left, right):
    return jnp.dot(left, right, preferred_element_type=F32)


def dot_nt(left, right):
    return lax.dot_general(left, right, NT, preferred_element_type=F32)


def hi_lo(value):
    high = value.astype(BF)
    return high, (value - high.astype(F32)).astype(BF)


def block_tile(blocks, low, quad, step):
    left = iota((16, 128), 1) < 64
    node = lax.shift_right_logical(iota((16, 128), 0), 2)
    none = jnp.zeros((16, 128), BF)
    lines = []
    for value in low:
        other = pltpu.roll(value.astype(F32), 64, 1).astype(BF)
        for even, odd in ((value, other), (other, value)):
            halves = []
            for part in range(2):
                is_even = jnp.logical_and(node == 2 * part, left)
                is_odd = jnp.logical_and(node == 2 * part + 1, jnp.logical_not(left))
                halves.append(jnp.where(is_even, even, jnp.where(is_odd, odd, none)))
            lines.append(jnp.concatenate(halves, 1))
    rows = pl.ds(pl.multiple_of(step * 256, 256), 256)
    weights = jnp.concatenate([blocks[2 * quad, rows, :], blocks[2 * quad + 1, rows, :]], 1)
    product = dot(jnp.concatenate(lines, 0), weights)
    results = []
    for half in range(2):
        columns = slice(128 * half, 128 * half + 128)
        first, second = product[32 * half : 32 * half + 16, columns], product[32 * half + 16 : 32 * half + 32, columns]
        results.append(jnp.where(left, first, second))
    return results


def relayout(raw, blocks, pair):
    def some_columns(group, carry):
        columns = pl.ds(pl.multiple_of(group * 16, 16), 16)
        cubes = []
        for half in range(2):
            for part in range(4):
                cube = jnp.stack([raw[2 * pair + half, 16 * part + a, columns, :] for a in range(16)], 0)
                cubes.append(jnp.transpose(cube, (1, 0, 2)))
        turned = [jnp.concatenate([cube[b] for cube in cubes], 0).T for b in range(16)]
        for part in range(8):
            cube = jnp.stack([one[16 * part : 16 * part + 16] for one in turned], 0)
            cube = jnp.transpose(cube, (1, 0, 2))
            for node in range(16):
                place = pl.multiple_of((part * 16 + node) * 64 + group * 16, 16)
                blocks[pair, pl.ds(place, 16), :] = cube[node]
        return carry

    lax.fori_loop(0, 4, some_columns, 0)


def kernel(
    stream_total,
    span_total,
    rhs_hbm, shift_hbm, diag_hbm, smooth_hbm, couple_hbm, coef_hbm, ids_hbm, cols_hbm, coarse_hbm, cshift_hbm,
    out_hbm,
    raw_rhs, raw_shift, raw_diag, raw_smooth, raw_couple, raw_coef, raw_ids, raw_cols, raw_coarse, raw_cshift,
    diag, smoother, rhs, shift, inverse, field, image, residual, low, wide, coef, couple,
    member, member_t, spread, pick, live, cshift, z_now, t_now, d_now, coarse_own, coarse_got,
    bound, bound_got, idpad,
    load_sem, halo_send, halo_recv, coarse_send, coarse_recv, bound_send, bound_recv, store_sem,
):
    position = lax.axis_index("stream")
    across = lax.axis_index("span")
    after = lax.rem(position + 1, stream_total)
    before = lax.rem(position + stream_total - 1, stream_total)
    right = lax.rem(across + 1, span_total)
    left = lax.rem(across + span_total - 1, span_total)
    group = min(8, stream_total)
    groups = stream_total // group

    stages = [[], [], []]
    for step in range(1, span_total):
        stages[0].append((position, lax.rem(across + step, span_total)))
    base = (position // group) * group
    for step in range(1, group):
        stages[1].append((base + lax.rem(position - base + step, group), across))
    for step in range(1, groups):
        stages[2].append((lax.rem(position + step * group, stream_total), across))
    partners = [who for stage in stages for who in stage]
    greeted = partners + [(after, across), (before, across)]

    @pl.when(position == 0)
    def _():
        for parity in range(2):
            wide[parity, 0] = jnp.zeros((WROWS, 128), BF)
            coarse_got[parity, 0] = jnp.zeros((128, 128), BF)

    @pl.when(position == stream_total - 1)
    def _():
        for parity in range(2):
            wide[parity, PAIRS + 1] = jnp.zeros((WROWS, 128), BF)
            coarse_got[parity, 1] = jnp.zeros((128, 128), BF)

    barrier = pltpu.get_barrier_semaphore()
    for who in greeted:
        pl.semaphore_signal(barrier, inc=1, device_id=who, device_id_type=MESH)

    loads = []

    def load(source, target):
        copy = pltpu.make_async_copy(source, target, load_sem.at[len(loads)])
        copy.start()
        loads.append(copy)
        return copy

    load_rhs = load(rhs_hbm, raw_rhs)
    load_shift = load(shift_hbm, raw_shift)
    load_ids = load(ids_hbm, raw_ids)
    load_cols = load(cols_hbm, raw_cols)
    load_cshift = load(cshift_hbm, raw_cshift)
    load_couple = load(couple_hbm, raw_couple)
    load_coef = load(coef_hbm, raw_coef)
    load_smooth = [
        load(smooth_hbm.at[pl.ds(2 * pair, 2)], raw_smooth.at[pl.ds(2 * pair, 2)]) for pair in range(PAIRS)
    ]
    load_coarse = load(coarse_hbm, raw_coarse)
    load_diag = [load(diag_hbm.at[pl.ds(2 * pair, 2)], raw_diag.at[pl.ds(2 * pair, 2)]) for pair in range(PAIRS)]

    def speed_of(place, extent):
        return jnp.sqrt(1.0 + 8.0 * (place + 0.5) / extent)

    here = position.astype(F32)
    coarse_speed = speed_of(jnp.full((1, 128), here, F32), float(stream_total))

    def spread_part(number, carry):
        rows = iota((128, 128), 0)
        lanes = iota((128, 128), 1)
        want = 2 * number + lax.shift_right_logical(rows, 6)
        spread[pl.ds(pl.multiple_of(number * 128, 128), 128), :] = one_zero((lanes & 63) == want)
        return carry

    lax.fori_loop(0, 32, spread_part, 0)

    load_rhs.wait()
    for pair in range(PAIRS):
        for vector in range(4):
            block = jnp.concatenate([raw_rhs[2 * pair, vector], raw_rhs[2 * pair + 1, vector]], 0)
            rhs[pair, pl.ds(vector, 128, stride=4), :] = block.T
    load_shift.wait()
    for pair in range(PAIRS):
        block = jnp.concatenate([raw_shift[2 * pair], raw_shift[2 * pair + 1]], 0).T
        for vector in range(4):
            shift[pair, pl.ds(vector, 128, stride=4), :] = block
        block = 1.0 / block
        for vector in range(4):
            inverse[pair, pl.ds(vector, 128, stride=4), :] = block

    load_ids.wait()
    idpad[...] = jnp.zeros(idpad.shape, BF)
    ids16 = jnp.concatenate([raw_ids[...].astype(F32), jnp.zeros((8, 128), F32)], 0).astype(BF)
    idpad[0:16, :] = ids16
    rows = iota((128, 128), 0)
    lanes = iota((128, 128), 1)
    expand = one_zero(lanes == lax.shift_right_logical(rows & 31, 2))
    by_slot = dot(expand, idpad[...])
    slot = (rows & 31).astype(F32)
    found = jnp.max(jnp.where(by_slot == slot, 1.0, 0.0), axis=1, keepdims=True)
    live[...] = jnp.broadcast_to(found, (128, 128))
    by_slot = by_slot.astype(BF)
    rows = iota((128, 512), 0)
    lanes = iota((128, 512), 1)
    node_of = one_zero(lax.shift_right_logical(lanes, 2) == rows)
    wide_ids = dot(by_slot, node_of)
    same = (lanes & 3) == lax.shift_right_logical(rows, 5)
    member[...] = one_zero(jnp.logical_and(wide_ids == (rows & 31).astype(F32), same))
    rows = iota((512, 128), 0)
    lanes = iota((512, 128), 1)
    of_node = one_zero(lax.shift_right_logical(rows, 2) == lanes)
    tall_ids = dot_nt(of_node, by_slot)
    same = (rows & 3) == lax.shift_right_logical(lanes, 5)
    member_t[...] = one_zero(jnp.logical_and(tall_ids == (lanes & 31).astype(F32), same))

    load_cols.wait()
    rows = iota((64, 32), 0)
    lanes = iota((64, 32), 1)
    repeat_rows = one_zero((rows & 31) == lanes)
    rows = iota((64, 64), 0)
    lanes = iota((64, 64), 1)
    same = lax.shift_right_logical(rows, 5) == lax.shift_right_logical(lanes, 5)
    for number in range(5):
        line = jnp.broadcast_to(raw_cols[number].astype(F32), (64, 32)).astype(BF)
        column = dot_nt(repeat_rows, line)
        pick[number] = one_zero(jnp.logical_and(column == (lanes & 31).astype(F32), same))

    load_cshift.wait()
    twice = jnp.where((iota((64, 128), 1) & 63) == iota((64, 128), 0), 1.0, 0.0)
    doubled = jnp.dot(raw_cshift[...], twice, precision=lax.Precision.HIGHEST, preferred_element_type=F32)
    for vector in range(4):
        cshift[32 * vector : 32 * vector + 32, :] = doubled

    load_couple.wait()
    for number in range(8):
        one = raw_couple[number].astype(F32)
        none = jnp.zeros((64, 64), F32)
        both = jnp.concatenate([jnp.concatenate([one, none], 1), jnp.concatenate([none, one], 1)], 0)
        couple[number * 128 : number * 128 + 128, :] = both.T.astype(BF)

    load_coef.wait()
    rows = iota((512, 128), 0)
    lanes = iota((512, 128), 1)
    of_node = one_zero(lax.shift_right_logical(rows, 2) == lanes)
    place = iota((8, 128), 0)
    node_speed = speed_of(here * 8.0 + place.astype(F32), float(stream_total * 8))
    for number in range(8):
        weights = node_speed * raw_coef[number]
        for half in range(2):
            lines = jnp.concatenate(
                [jnp.broadcast_to(weights[4 * half + i : 4 * half + i + 1, :], (64, 128)) for i in range(4)], 0
            ).astype(BF)
            laid = dot_nt(of_node, lines).astype(BF)
            coef[number, 2 * half] = laid[:, :128]
            coef[number, 2 * half + 1] = laid[:, 128:]

    pl.semaphore_wait(barrier, len(greeted))

    bound_copies = [
        pltpu.make_async_remote_copy(
            src_ref=bound.at[stage],
            dst_ref=bound_got.at[slot_number],
            send_sem=bound_send.at[slot_number],
            recv_sem=bound_recv.at[slot_number],
            device_id=who,
            device_id_type=MESH,
        )
        for slot_number, (stage, who) in enumerate(
            [(stage, who) for stage in range(3) for who in stages[stage]]
        )
    ]
    starts = [0, len(stages[0]), len(stages[0]) + len(stages[1]), len(partners)]

    def bound_begin(stage):
        for number in range(starts[stage], starts[stage + 1]):
            bound_copies[number].start()

    def bound_end(stage):
        value = bound[stage]
        for number in range(starts[stage], starts[stage + 1]):
            bound_copies[number].wait()
            value = jnp.maximum(value, bound_got[number])
        bound[stage + 1] = value

    def coarse_bound():
        load_coarse.wait()
        total = jnp.zeros((64, 128), F32)
        for number in range(32):
            columns = slice(128 * number, 128 * number + 128)
            size = jnp.abs(raw_coarse[0, :, columns])
            for kind in range(1, 5):
                size = size + jnp.abs(raw_coarse[kind, :, columns])
            high, rest = hi_lo(size)
            total = total + dot(jnp.concatenate([high, rest], 0), spread[columns, :])
        largest = live[0:32, :] * (cshift[0:32, :] + coarse_speed * (total[0:32] + total[32:64]))
        bound[0] = jnp.broadcast_to(jnp.max(jnp.max(largest, axis=1, keepdims=True), axis=0, keepdims=True), (8, 128))

    def begin(copies):
        for copy in copies[2:]:
            copy.start()
        pl.when(position < stream_total - 1)(copies[0].start)
        pl.when(position > 0)(copies[1].start)

    def arrived(copies):
        for copy in copies[2:]:
            copy.wait_recv()
        pl.when(position < stream_total - 1)(copies[1].wait_recv)
        pl.when(position > 0)(copies[0].wait_recv)

    def departed(copies):
        for copy in copies[2:]:
            copy.wait_send()
        pl.when(position < stream_total - 1)(copies[0].wait_send)
        pl.when(position > 0)(copies[1].wait_send)

    def halo_copies(parity, half):
        def copy(number, source, target, who):
            return pltpu.make_async_remote_copy(
                src_ref=source,
                dst_ref=target,
                send_sem=halo_send.at[parity, half, number],
                recv_sem=halo_recv.at[parity, half, number],
                device_id=who,
                device_id_type=MESH,
            )

        mine = pl.ds(pl.multiple_of(EDGE + half * (ROWS // 2), 16), ROWS // 2)
        inner = pl.ds(1, PAIRS)
        edge = pl.ds(pl.multiple_of(EDGE + half * (ROWS - EDGE), 16), EDGE)
        beyond = pl.ds(pl.multiple_of((1 - half) * (ROWS + EDGE), 16), EDGE)
        beside = lax.rem(across + span_total - 1 + 2 * half, span_total)
        return [
            copy(0, wide.at[parity, PAIRS, mine], wide.at[parity, 0, mine], (after, across)),
            copy(1, wide.at[parity, 1, mine], wide.at[parity, PAIRS + 1, mine], (before, across)),
            copy(2, wide.at[parity, inner, edge], wide.at[parity, inner, beyond], (position, beside)),
        ]

    def smooth_step(parity, more):
        following = 1 - parity

        def tiles(part, carry):
            for inside in range(32):
                quad, step = inside % 2, part * 16 + inside // 2
                rows = pl.ds(pl.multiple_of(step * 16, 16), 16)
                shifted = pl.ds(pl.multiple_of(step * 16 + EDGE, 16), 16)
                operand = [low[2 * quad + half, rows, :] for half in range(2)]
                parts = block_tile(smoother, operand, quad, step)
                for half in range(2):
                    pair = 2 * quad + half
                    change = residual[pair, rows, :] * inverse[pair, rows, :] + parts[half]
                    value = field[pair, rows, :] + OMEGA * change
                    field[pair, rows, :] = value
                    wide[following, pair + 1, shifted, :] = value.astype(BF)

            @pl.when(more)
            def _():
                begin(halo_copies(following, part))

            return carry

        lax.fori_loop(0, 2, tiles, 0)

    def operator_inner(parity):
        def tiles(part, carry):
            for inside in range(32):
                quad, step = inside % 2, part * 16 + inside // 2
                rows = pl.ds(pl.multiple_of(step * 16, 16), 16)
                shifted = pl.ds(pl.multiple_of(step * 16 + EDGE, 16), 16)
                operand = [wide[parity, 2 * quad + half + 1, shifted, :] for half in range(2)]
                parts = block_tile(diag, operand, quad, step)
                for half in range(2):
                    pair = 2 * quad + half
                    image[pair, rows, :] = shift[pair, rows, :] * operand[half].astype(F32) + parts[half]
            return carry

        lax.fori_loop(0, 2, tiles, 0)

    def operator_outer(parity, scale):
        left_half = iota((128, 128), 1) < 64

        def chunk(pair, start):
            rows = pl.ds(pl.multiple_of(start, 128), 128)

            def at(which):
                return wide[parity, which, pl.ds(pl.multiple_of(start + EDGE, 16), 128), :]

            here_now, lower, upper = at(pair + 1), at(pair), at(pair + 2)
            around = wide[parity, pair + 1, pl.ds(pl.multiple_of(start, 16), 128 + 2 * EDGE), :]
            shifted = [
                lower,
                pltpu.roll(jnp.where(left_half, here_now, lower).astype(F32), 64, 1).astype(BF),
                pltpu.roll(jnp.where(left_half, upper, here_now).astype(F32), 64, 1).astype(BF),
                upper,
                around[EDGE - 8 : EDGE + 120],
                around[EDGE - 4 : EDGE + 124],
                around[EDGE + 4 : EDGE + 132],
                around[EDGE + 8 : EDGE + 136],
            ]
            operand = jnp.concatenate([coef[m, pair, rows, :] * shifted[m] for m in range(8)], 1)
            value = scale * rhs[pair, rows, :] - (image[pair, rows, :] + dot(operand, couple[...]))
            residual[pair, rows, :] = value
            low[pair, rows, :] = value.astype(BF)

        for pair in (1, 2):
            for start in (128, 256):
                chunk(pair, start)
        for half in range(2):
            arrived(halo_copies(parity, half))

        def chunks(number, carry):
            mixed = number // 2
            for inside in range(4):
                pair = mixed * (1 + inside // 2) + (1 - mixed) * 3 * number
                chunk(pair, 128 * (mixed * 3 * (inside % 2) + (1 - mixed) * inside))
            return carry

        lax.fori_loop(0, 3, chunks, 0)

    def coarse_copies(parity, half):
        targets = [(after, across), (before, across), (position, right), (position, left)]
        rows = pl.ds(64 * half, 64)
        return [
            pltpu.make_async_remote_copy(
                src_ref=coarse_own.at[parity, rows],
                dst_ref=coarse_got.at[parity, number, rows],
                send_sem=coarse_send.at[parity, half, number],
                recv_sem=coarse_recv.at[parity, half, number],
                device_id=who,
                device_id_type=MESH,
            )
            for number, who in enumerate(targets)
        ]

    def restrict():
        total = jnp.zeros((128, 512), F32)
        parts = []
        for pair in range(PAIRS):
            high, rest = hi_lo(residual[pair])
            parts.append(dot(member[...], high) + dot(member[...], rest))
        left_half = iota((8, 128), 1) < 64
        top = iota((8, 128), 0) < 4
        for vector in range(4):
            for pair in range(PAIRS):
                begin = 32 * vector + 8 * pair
                own = jnp.where(top == left_half, parts[pair][begin : begin + 8, :], 0.0)
                t_now[begin : begin + 8, :] = own + pltpu.roll(own, 64, 1)

    def coarse_product(got):
        near = []
        for number in range(5):
            value = dot(pick[number], got[number])
            near.append(value + pltpu.roll(value, 64, 1))
        total = jnp.zeros((64, 128), F32)
        for column in range(16):
            sides = []
            for side in range(2):
                begin_at = 256 * column + 128 * side
                blocks = [raw_coarse[k, :, begin_at : begin_at + 128] for k in range(5)]
                pieces = []
                for vector in range(2):
                    rows = slice(32 * vector, 32 * vector + 32)
                    part = blocks[0] * near[0][rows]
                    for k in range(1, 5):
                        part = part + blocks[k] * near[k][rows]
                    pieces.append(part.astype(BF))
                sides.append(jnp.concatenate(pieces, 0))
            total = total + dot(jnp.concatenate(sides, 1), spread[256 * column : 256 * column + 256, :])
        return total

    def coarse_solve():
        upper_edge = 1.05 * bound[3]
        lower_edge = upper_edge / 20.0
        middle = 0.5 * (upper_edge + lower_edge)
        gap = 0.5 * (upper_edge - lower_edge)
        sigma = middle / gap
        left_half = iota((64, 128), 1) < 64
        halves = [slice(0, 64), slice(64, 128)]

        def send(parity, half, direction):
            high, rest = hi_lo(direction)
            coarse_own[parity, halves[half], :] = jnp.where(left_half, high, rest)
            begin(coarse_copies(parity, half))

        restrict()
        for half in range(2):
            direction = t_now[halves[half], :] / middle[0:1, :]
            send(0, half, direction)
            d_now[halves[half], :] = direction
            z_now[halves[half], :] = direction

        def step(number, rho):
            parity = lax.rem(number, 2)
            rho_next = 1.0 / (2.0 * sigma - rho)
            for half in range(2):
                rows = halves[half]
                arrived(coarse_copies(parity, half))
                got = [coarse_own[parity, rows, :]] + [coarse_got[parity, k, rows, :] for k in range(4)]
                coupled = coarse_product(got)
                direction = d_now[rows, :]
                t_next = t_now[rows, :] - live[rows, :] * (cshift[rows, :] * direction + coarse_speed * coupled)
                t_now[rows, :] = t_next
                direction = (rho_next * rho)[0:1, :] * direction + (2.0 * rho_next / gap)[0:1, :] * t_next

                @pl.when(jnp.logical_and(number > 0, number < CHEB - 2))
                def _():
                    departed(coarse_copies(1 - parity, half))

                @pl.when(number < CHEB - 2)
                def _():
                    send(1 - parity, half, direction)

                d_now[rows, :] = direction
                z_now[rows, :] = z_now[rows, :] + direction
            return rho_next

        lax.fori_loop(0, CHEB - 1, step, 1.0 / sigma)
        for parity in range(2):
            for half in range(2):
                departed(coarse_copies(parity, half))

    def prolong(parity):
        following = 1 - parity
        slots = lax.shift_right_logical(iota((128, 128), 0) & 31, 2)
        half = lax.shift_right_logical(iota((128, 128), 1), 6)
        twice = jnp.concatenate([member_t[...], member_t[...]], 1)
        for pair in range(PAIRS):
            high, rest = hi_lo(jnp.where(slots == 2 * pair + half, z_now[...], 0.0))
            value = dot(twice, jnp.concatenate([high, rest], 0))
            field[pair] = field[pair] + value
            wide[following, pair + 1, EDGE : EDGE + ROWS, :] = value.astype(BF)

    field[...] = jnp.zeros(field.shape, F32)
    for pair in range(PAIRS):
        residual[pair] = rhs[pair]
        low[pair] = rhs[pair].astype(BF)

    def round_of(number, carry):
        parity = lax.rem(number, 2)

        @pl.when(number == 0)
        def _():
            for pair in range(PAIRS):
                load_smooth[pair].wait()
                relayout(raw_smooth, smoother, pair)
            coarse_bound()
            bound_begin(0)

        @pl.when(number > 0)
        def _():
            operator_inner(parity)
            scale = jnp.where(number == 3, 0.0, 1.0)
            operator_outer(parity, scale)
            for half in range(2):
                departed(halo_copies(parity, half))

        @pl.when(number == 2)
        def _():
            bound_end(2)
            coarse_solve()
            prolong(parity)
            for half in range(2):
                begin(halo_copies(1 - parity, half))

        @pl.when(number != 2)
        def _():
            smooth_step(parity, number < 5)

        @pl.when(number == 0)
        def _():
            bound_end(0)
            bound_begin(1)
            for pair in range(PAIRS):
                load_diag[pair].wait()
                relayout(raw_diag, diag, pair)

        @pl.when(number == 1)
        def _():
            bound_end(1)
            bound_begin(2)

        return carry

    lax.fori_loop(0, 6, round_of, 0)

    stores = []
    for pair in range(PAIRS):
        for vector in range(4):
            block = field[pair, pl.ds(vector, 128, stride=4), :].T
            raw_rhs[2 * pair, vector] = block[0:64]
            raw_rhs[2 * pair + 1, vector] = block[64:128]
        copy = pltpu.make_async_copy(
            raw_rhs.at[pl.ds(2 * pair, 2)], out_hbm.at[pl.ds(2 * pair, 2)], store_sem.at[pair]
        )
        copy.start()
        stores.append(copy)
    for copy in stores:
        copy.wait()


def local(stream_total, span_total, right_side, shift_fine, diag_blocks, smoother, couplings, coefficients,
          agg_ids, coarse_columns, coarse_blocks, coarse_shift):
    columns = jnp.transpose(coarse_columns, (0, 3, 1, 2))[0]
    blocks = jnp.transpose(coarse_blocks[0, 0], (1, 0, 2))
    vm = pltpu.VMEM
    dma = pltpu.SemaphoreType.DMA
    partners = (span_total - 1) + (min(8, stream_total) - 1) + (stream_total // min(8, stream_total) - 1)
    shape = (PAIRS, ROWS, 128)
    scratch = [
        vm((8, 4, 64, 128), F32), vm((8, 64, 128), F32), vm((8, 64, 64, 128), BF), vm((8, 64, 64, 128), BF),
        vm((8, 64, 64), BF), vm((8, 8, 128), F32), vm((8, 128), jnp.int32), vm((5, 1, 32), jnp.int32),
        vm((5, 32, 4096), F32), vm((32, 64), F32),
        vm((PAIRS, 8192, 128), BF), vm((PAIRS, 8192, 128), BF), vm(shape, F32), vm(shape, F32), vm(shape, F32),
        vm(shape, F32), vm(shape, F32), vm(shape, F32), vm(shape, BF), vm((2, PAIRS + 2, WROWS, 128), BF),
        vm((8,) + shape, BF), vm((1024, 128), BF),
        vm((128, 512), BF), vm((512, 128), BF), vm((4096, 128), BF), vm((5, 64, 64), BF), vm((128, 128), F32),
        vm((128, 128), F32), vm((128, 128), F32), vm((128, 128), F32), vm((128, 128), F32),
        vm((2, 128, 128), BF), vm((2, 4, 128, 128), BF),
        vm((4, 8, 128), F32), vm((partners, 8, 128), F32), vm((128, 128), BF),
        dma((16,)), dma((2, 2, 3)), dma((2, 2, 3)), dma((2, 2, 4)), dma((2, 2, 4)), dma((partners,)), dma((partners,)), dma((4,)),
    ]
    anywhere = pl.BlockSpec(memory_space=pl.ANY)
    return pl.pallas_call(
        functools.partial(kernel, stream_total, span_total),
        out_shape=jax.ShapeDtypeStruct(right_side.shape, F32),
        in_specs=[anywhere] * 10,
        out_specs=anywhere,
        scratch_shapes=scratch,
        compiler_params=pltpu.CompilerParams(
            collective_id=0, has_side_effects=True, vmem_limit_bytes=60 * 1024 * 1024
        ),
        name="cycle",
    )(right_side, shift_fine, diag_blocks, smoother, couplings, coefficients, agg_ids, columns, blocks,
      coarse_shift[0, 0])


def solution(mesh):
    return jax.shard_map(
        functools.partial(local, mesh.shape["stream"], mesh.shape["span"]),
        mesh=mesh,
        in_specs=(
            P("stream", None, None, "span"),
            P("stream", None, "span"),
            P("stream", None, None, "span"),
            P("stream", None, None, "span"),
            P(),
            P(None, "stream", "span"),
            P("stream", "span"),
            P("stream", "span", None, None),
            P("stream", "span", None, None, None),
            P("stream", "span", None, None),
        ),
        out_specs=P("stream", None, None, "span"),
        check_vma=False,
    )
```

```python
import functools

import jax
import jax.numpy as jnp
from jax import lax
from jax.experimental import pallas as pl
from jax.experimental.pallas import tpu as pltpu
from jax.sharding import PartitionSpec as P

OMEGA = 0.3
CHEB = 8
BF = jnp.bfloat16
F32 = jnp.float32
MESH = pl.DeviceIdType.MESH
NT = (((1,), (1,)), ((), ()))
PAIRS = 4
QUADS = ((0, 3), (1, 2))
ROWS = 512
EDGE = 16
WROWS = ROWS + 2 * EDGE


def iota(shape, dim):
    return lax.broadcasted_iota(jnp.int32, shape, dim)


def one_zero(mask):
    return jnp.where(mask, 1.0, 0.0).astype(BF)


def dot(left, right):
    return jnp.dot(left, right, preferred_element_type=F32)


def dot_nt(left, right):
    return lax.dot_general(left, right, NT, preferred_element_type=F32)


def hi_lo(value):
    high = value.astype(BF)
    return high, (value - high.astype(F32)).astype(BF)


def block_tile(blocks, low, quad, step):
    left = iota((16, 128), 1) < 64
    node = lax.shift_right_logical(iota((16, 128), 0), 2)
    none = jnp.zeros((16, 128), BF)
    lines = []
    for value in low:
        other = pltpu.roll(value.astype(F32), 64, 1).astype(BF)
        for even, odd in ((value, other), (other, value)):
            halves = []
            for part in range(2):
                is_even = jnp.logical_and(node == 2 * part, left)
                is_odd = jnp.logical_and(node == 2 * part + 1, jnp.logical_not(left))
                halves.append(jnp.where(is_even, even, jnp.where(is_odd, odd, none)))
            lines.append(jnp.concatenate(halves, 1))
    rows = pl.ds(pl.multiple_of(step * 256, 256), 256)
    weights = jnp.concatenate([blocks[pair, rows, :] for pair in QUADS[quad]], 1)
    product = dot(jnp.concatenate(lines, 0), weights)
    results = []
    for half in range(2):
        columns = slice(128 * half, 128 * half + 128)
        first, second = product[32 * half : 32 * half + 16, columns], product[32 * half + 16 : 32 * half + 32, columns]
        results.append(jnp.where(left, first, second))
    return results


def relayout(raw, blocks, pair):
    def some_columns(group, carry):
        columns = pl.ds(pl.multiple_of(group * 16, 16), 16)
        cubes = []
        for half in range(2):
            for part in range(4):
                cube = jnp.stack([raw[2 * pair + half, 16 * part + a, columns, :] for a in range(16)], 0)
                cubes.append(jnp.transpose(cube, (1, 0, 2)))
        turned = [jnp.concatenate([cube[b] for cube in cubes], 0).T for b in range(16)]
        for part in range(8):
            cube = jnp.stack([one[16 * part : 16 * part + 16] for one in turned], 0)
            cube = jnp.transpose(cube, (1, 0, 2))
            for node in range(16):
                place = pl.multiple_of((part * 16 + node) * 64 + group * 16, 16)
                blocks[pair, pl.ds(place, 16), :] = cube[node]
        return carry

    lax.fori_loop(0, 4, some_columns, 0, unroll=2)


def kernel(
    stream_total,
    span_total,
    rhs_hbm, shift_hbm, diag_hbm, smooth_hbm, couple_hbm, coef_hbm, ids_hbm, cols_hbm, coarse_hbm, cshift_hbm,
    out_hbm,
    raw_rhs, raw_shift, raw_diag, raw_smooth, raw_couple, raw_coef, raw_ids, raw_cols, raw_coarse, raw_cshift,
    diag, smoother, rhs, shift, inverse, field, image, residual, low, wide, coef, couple,
    member, member_t, spread, pick, live, cshift, z_now, t_now, d_now, coarse_own, coarse_got,
    bound, bound_got, idpad, by_node,
    load_sem, halo_send, halo_recv, span_send, span_recv, coarse_send, coarse_recv, bound_send, bound_recv, store_sem,
):
    position = lax.axis_index("stream")
    across = lax.axis_index("span")
    after = lax.rem(position + 1, stream_total)
    before = lax.rem(position + stream_total - 1, stream_total)
    right = lax.rem(across + 1, span_total)
    left = lax.rem(across + span_total - 1, span_total)
    group = min(8, stream_total)
    groups = stream_total // group

    stages = [[], [], []]
    for step in range(1, span_total):
        stages[0].append((position, lax.rem(across + step, span_total)))
    base = (position // group) * group
    for step in range(1, group):
        stages[1].append((base + lax.rem(position - base + step, group), across))
    for step in range(1, groups):
        stages[2].append((lax.rem(position + step * group, stream_total), across))
    partners = [who for stage in stages for who in stage]
    greeted = partners + [(after, across), (before, across)]

    @pl.when(position == 0)
    def _():
        for parity in range(2):
            wide[parity, 0] = jnp.zeros((WROWS, 128), BF)
            coarse_got[parity, 0] = jnp.zeros((128, 128), BF)

    @pl.when(position == stream_total - 1)
    def _():
        for parity in range(2):
            wide[parity, PAIRS + 1] = jnp.zeros((WROWS, 128), BF)
            coarse_got[parity, 1] = jnp.zeros((128, 128), BF)

    barrier = pltpu.get_barrier_semaphore()
    for who in greeted:
        pl.semaphore_signal(barrier, inc=1, device_id=who, device_id_type=MESH)

    loads = []

    def load(source, target):
        copy = pltpu.make_async_copy(source, target, load_sem.at[len(loads)])
        copy.start()
        loads.append(copy)
        return copy

    load_rhs = load(rhs_hbm, raw_rhs)
    load_shift = load(shift_hbm, raw_shift)
    load_ids = load(ids_hbm, raw_ids)
    load_cols = load(cols_hbm, raw_cols)
    load_cshift = load(cshift_hbm, raw_cshift)
    load_couple = load(couple_hbm, raw_couple)
    load_coef = load(coef_hbm, raw_coef)
    load_smooth = [
        load(smooth_hbm.at[pl.ds(2 * pair, 2)], raw_smooth.at[pl.ds(2 * pair, 2)]) for pair in range(PAIRS)
    ]
    load_coarse = load(coarse_hbm, raw_coarse)
    load_diag = [load(diag_hbm.at[pl.ds(2 * pair, 2)], raw_diag.at[pl.ds(2 * pair, 2)]) for pair in range(PAIRS)]

    def speed_of(place, extent):
        return jnp.sqrt(1.0 + 8.0 * (place + 0.5) / extent)

    here = position.astype(F32)
    coarse_speed = speed_of(jnp.full((1, 128), here, F32), float(stream_total))

    def spread_part(number, carry):
        rows = iota((128, 128), 0)
        lanes = iota((128, 128), 1)
        want = 2 * number + lax.shift_right_logical(rows, 6)
        spread[pl.ds(pl.multiple_of(number * 128, 128), 128), :] = one_zero((lanes & 63) == want)
        return carry

    lax.fori_loop(0, 32, spread_part, 0)

    load_rhs.wait()
    for pair in range(PAIRS):
        for vector in range(4):
            block = jnp.concatenate([raw_rhs[2 * pair, vector], raw_rhs[2 * pair + 1, vector]], 0)
            rhs[pair, pl.ds(vector, 128, stride=4), :] = block.T
    load_shift.wait()
    for pair in range(PAIRS):
        block = jnp.concatenate([raw_shift[2 * pair], raw_shift[2 * pair + 1]], 0).T
        for vector in range(4):
            shift[pair, pl.ds(vector, 128, stride=4), :] = block
        block = 1.0 / block
        for vector in range(4):
            inverse[pair, pl.ds(vector, 128, stride=4), :] = block

    load_ids.wait()
    idpad[...] = jnp.zeros(idpad.shape, BF)
    ids16 = jnp.concatenate([raw_ids[...].astype(F32), jnp.zeros((8, 128), F32)], 0).astype(BF)
    idpad[0:16, :] = ids16
    rows = iota((128, 128), 0)
    lanes = iota((128, 128), 1)
    expand = one_zero(lanes == lax.shift_right_logical(rows & 31, 2))
    by_slot = dot(expand, idpad[...])
    slot = (rows & 31).astype(F32)
    found = jnp.max(jnp.where(by_slot == slot, 1.0, 0.0), axis=1, keepdims=True)
    live[...] = jnp.broadcast_to(found, (128, 128))
    by_node[...] = by_slot.astype(BF)

    load_cshift.wait()
    twice = jnp.where((iota((64, 128), 1) & 63) == iota((64, 128), 0), 1.0, 0.0)
    doubled = jnp.dot(raw_cshift[...], twice, precision=lax.Precision.HIGHEST, preferred_element_type=F32)
    for vector in range(4):
        cshift[32 * vector : 32 * vector + 32, :] = doubled

    load_couple.wait()
    for number in range(8):
        one = raw_couple[number].astype(F32)
        none = jnp.zeros((64, 64), F32)
        both = jnp.concatenate([jnp.concatenate([one, none], 1), jnp.concatenate([none, one], 1)], 0)
        couple[number * 128 : number * 128 + 128, :] = both.T.astype(BF)

    load_coef.wait()
    rows = iota((512, 128), 0)
    lanes = iota((512, 128), 1)
    of_node = one_zero(lax.shift_right_logical(rows, 2) == lanes)
    place = iota((8, 128), 0)
    node_speed = speed_of(here * 8.0 + place.astype(F32), float(stream_total * 8))
    for number in range(8):
        weights = node_speed * raw_coef[number]
        for half in range(2):
            lines = jnp.concatenate(
                [jnp.broadcast_to(weights[4 * half + i : 4 * half + i + 1, :], (64, 128)) for i in range(4)], 0
            ).astype(BF)
            laid = dot_nt(of_node, lines).astype(BF)
            coef[number, 2 * half] = laid[:, :128]
            coef[number, 2 * half + 1] = laid[:, 128:]

    def member_table():
        rows = iota((128, 512), 0)
        lanes = iota((128, 512), 1)
        node_of = one_zero(lax.shift_right_logical(lanes, 2) == rows)
        wide_ids = dot(by_node[...], node_of)
        same = (lanes & 3) == lax.shift_right_logical(rows, 5)
        member[...] = one_zero(jnp.logical_and(wide_ids == (rows & 31).astype(F32), same))

    def coarse_tables():
        rows = iota((512, 128), 0)
        lanes = iota((512, 128), 1)
        of_node = one_zero(lax.shift_right_logical(rows, 2) == lanes)
        tall_ids = dot_nt(of_node, by_node[...])
        same = (rows & 3) == lax.shift_right_logical(lanes, 5)
        member_t[...] = one_zero(jnp.logical_and(tall_ids == (lanes & 31).astype(F32), same))

        load_cols.wait()
        rows = iota((64, 32), 0)
        lanes = iota((64, 32), 1)
        repeat_rows = one_zero((rows & 31) == lanes)
        rows = iota((64, 64), 0)
        lanes = iota((64, 64), 1)
        same = lax.shift_right_logical(rows, 5) == lax.shift_right_logical(lanes, 5)
        for number in range(5):
            line = jnp.broadcast_to(raw_cols[number].astype(F32), (64, 32)).astype(BF)
            column = dot_nt(repeat_rows, line)
            pick[number] = one_zero(jnp.logical_and(column == (lanes & 31).astype(F32), same))

    pl.semaphore_wait(barrier, len(greeted))

    bound_copies = [
        pltpu.make_async_remote_copy(
            src_ref=bound.at[stage],
            dst_ref=bound_got.at[slot_number],
            send_sem=bound_send.at[slot_number],
            recv_sem=bound_recv.at[slot_number],
            device_id=who,
            device_id_type=MESH,
        )
        for slot_number, (stage, who) in enumerate(
            [(stage, who) for stage in range(3) for who in stages[stage]]
        )
    ]
    starts = [0, len(stages[0]), len(stages[0]) + len(stages[1]), len(partners)]

    def bound_begin(stage):
        for number in range(starts[stage], starts[stage + 1]):
            bound_copies[number].start()

    def bound_end(stage):
        value = bound[stage]
        for number in range(starts[stage], starts[stage + 1]):
            bound_copies[number].wait()
            value = jnp.maximum(value, bound_got[number])
        bound[stage + 1] = value

    def coarse_bound():
        load_coarse.wait()
        total = jnp.zeros((64, 128), F32)
        for number in range(32):
            columns = slice(128 * number, 128 * number + 128)
            size = jnp.abs(raw_coarse[0, :, columns])
            for kind in range(1, 5):
                size = size + jnp.abs(raw_coarse[kind, :, columns])
            high, rest = hi_lo(size)
            total = total + dot(jnp.concatenate([high, rest], 0), spread[columns, :])
        largest = live[0:32, :] * (cshift[0:32, :] + coarse_speed * (total[0:32] + total[32:64]))
        bound[0] = jnp.broadcast_to(jnp.max(jnp.max(largest, axis=1, keepdims=True), axis=0, keepdims=True), (8, 128))

    def begin(copies):
        for copy in copies[2:]:
            copy.start()
        pl.when(position < stream_total - 1)(copies[0].start)
        pl.when(position > 0)(copies[1].start)

    def arrived(copies):
        for copy in copies[2:]:
            copy.wait_recv()
        pl.when(position < stream_total - 1)(copies[1].wait_recv)
        pl.when(position > 0)(copies[0].wait_recv)

    def departed(copies):
        for copy in copies[2:]:
            copy.wait_send()
        pl.when(position < stream_total - 1)(copies[0].wait_send)
        pl.when(position > 0)(copies[1].wait_send)

    def halo_copy(source, target, send_sem, recv_sem, who):
        return pltpu.make_async_remote_copy(
            src_ref=source, dst_ref=target, send_sem=send_sem, recv_sem=recv_sem, device_id=who, device_id_type=MESH
        )

    def stream_copies(parity, half):
        mine = pl.ds(pl.multiple_of(EDGE + half * (ROWS // 2), 16), ROWS // 2)
        ends = [(PAIRS, 0, after), (1, PAIRS + 1, before)]
        return [
            halo_copy(
                wide.at[parity, source, mine], wide.at[parity, target, mine],
                halo_send.at[parity, half, number], halo_recv.at[parity, half, number], (who, across),
            )
            for number, (source, target, who) in enumerate(ends)
        ]

    def span_copies(parity):
        inner = pl.ds(1, PAIRS)
        ends = [(ROWS, 0, right), (EDGE, ROWS + EDGE, left)]
        return [
            halo_copy(
                wide.at[parity, inner, pl.ds(source, EDGE)], wide.at[parity, inner, pl.ds(target, EDGE)],
                span_send.at[parity, number], span_recv.at[parity, number], (position, who),
            )
            for number, (source, target, who) in enumerate(ends)
        ]

    def span_begin(parity):
        for copy in span_copies(parity):
            copy.start()

    def halo_departed(parity):
        for half in range(2):
            departed(stream_copies(parity, half))
        for copy in span_copies(parity):
            copy.wait_send()

    def result_copy(pair):
        return pltpu.make_async_copy(field.at[pair], out_hbm.at[pair], store_sem.at[pair])

    def smooth_step(parity, more):
        following = 1 - parity

        def tile(quad, step):
            rows = pl.ds(pl.multiple_of(step * 16, 16), 16)
            shifted = pl.ds(pl.multiple_of(step * 16 + EDGE, 16), 16)
            parts = block_tile(smoother, [low[pair, rows, :] for pair in QUADS[quad]], quad, step)
            for pair, part in zip(QUADS[quad], parts):
                change = residual[pair, rows, :] * inverse[pair, rows, :] + part
                value = field[pair, rows, :] + OMEGA * change
                field[pair, rows, :] = value
                wide[following, pair + 1, shifted, :] = value.astype(BF)

        def outside(half, carry):
            for inside in range(16):
                tile(0, half * 16 + inside)

            @pl.when(more)
            def _():
                begin(stream_copies(following, half))

            return carry

        def inside_of(half, carry):
            for inside in range(15):
                tile(1, half * 15 + 1 + inside)
            return carry

        lax.fori_loop(0, 2, outside, 0)

        @pl.when(jnp.logical_not(more))
        def _():
            for pair in QUADS[0]:
                result_copy(pair).start()

        for step in (0, 31):
            tile(1, step)

        @pl.when(more)
        def _():
            span_begin(following)

        lax.fori_loop(0, 2, inside_of, 0)

    def operator_inner(parity):
        def tiles(part, carry):
            for inside in range(32):
                quad, step = inside % 2, part * 16 + inside // 2
                rows = pl.ds(pl.multiple_of(step * 16, 16), 16)
                shifted = pl.ds(pl.multiple_of(step * 16 + EDGE, 16), 16)
                operand = [wide[parity, pair + 1, shifted, :] for pair in QUADS[quad]]
                parts = block_tile(diag, operand, quad, step)
                for pair, value, part_of in zip(QUADS[quad], operand, parts):
                    image[pair, rows, :] = shift[pair, rows, :] * value.astype(F32) + part_of
            return carry

        lax.fori_loop(0, 2, tiles, 0)

    def operator_outer(parity, scale):
        def chunk(pair, start, size):
            left_half = iota((size, 128), 1) < 64
            rows = pl.ds(pl.multiple_of(start, 128), size)

            def at(which):
                return wide[parity, which, pl.ds(pl.multiple_of(start + EDGE, 16), size), :]

            here_now, lower, upper = at(pair + 1), at(pair), at(pair + 2)
            around = wide[parity, pair + 1, pl.ds(pl.multiple_of(start, 16), size + 2 * EDGE), :]
            shifted = [
                lower,
                pltpu.roll(jnp.where(left_half, here_now, lower).astype(F32), 64, 1).astype(BF),
                pltpu.roll(jnp.where(left_half, upper, here_now).astype(F32), 64, 1).astype(BF),
                upper,
                around[EDGE - 8 : EDGE - 8 + size],
                around[EDGE - 4 : EDGE - 4 + size],
                around[EDGE + 4 : EDGE + 4 + size],
                around[EDGE + 8 : EDGE + 8 + size],
            ]
            operand = jnp.concatenate([coef[m, pair, rows, :] * shifted[m] for m in range(8)], 1)
            value = scale * rhs[pair, rows, :] - (image[pair, rows, :] + dot(operand, couple[...]))
            residual[pair, rows, :] = value
            low[pair, rows, :] = value.astype(BF)

        for pair in (1, 2):
            chunk(pair, 128, 256)
        for copy in span_copies(parity):
            copy.wait_recv()
        for pair in (1, 2):
            for start in (0, 384):
                chunk(pair, start, 128)
        for half in range(2):
            arrived(stream_copies(parity, half))

        def outer_pairs(number, carry):
            for start in (0, 256):
                chunk(3 * number, start, 256)
            return carry

        lax.fori_loop(0, 2, outer_pairs, 0)

    def coarse_copies(parity, half):
        targets = [(after, across), (before, across), (position, right), (position, left)]
        rows = pl.ds(64 * half, 64)
        return [
            pltpu.make_async_remote_copy(
                src_ref=coarse_own.at[parity, rows],
                dst_ref=coarse_got.at[parity, number, rows],
                send_sem=coarse_send.at[parity, half, number],
                recv_sem=coarse_recv.at[parity, half, number],
                device_id=who,
                device_id_type=MESH,
            )
            for number, who in enumerate(targets)
        ]

    def restrict():
        total = jnp.zeros((128, 512), F32)
        parts = []
        for pair in range(PAIRS):
            high, rest = hi_lo(residual[pair])
            parts.append(dot(member[...], high) + dot(member[...], rest))
        left_half = iota((8, 128), 1) < 64
        top = iota((8, 128), 0) < 4
        for vector in range(4):
            for pair in range(PAIRS):
                begin = 32 * vector + 8 * pair
                own = jnp.where(top == left_half, parts[pair][begin : begin + 8, :], 0.0)
                t_now[begin : begin + 8, :] = own + pltpu.roll(own, 64, 1)

    def coarse_product(got):
        near = []
        for number in range(5):
            value = dot(pick[number], got[number])
            near.append(value + pltpu.roll(value, 64, 1))
        total = jnp.zeros((64, 128), F32)
        for column in range(16):
            sides = []
            for side in range(2):
                begin_at = 256 * column + 128 * side
                blocks = [raw_coarse[k, :, begin_at : begin_at + 128] for k in range(5)]
                pieces = []
                for vector in range(2):
                    rows = slice(32 * vector, 32 * vector + 32)
                    part = blocks[0] * near[0][rows]
                    for k in range(1, 5):
                        part = part + blocks[k] * near[k][rows]
                    pieces.append(part.astype(BF))
                sides.append(jnp.concatenate(pieces, 0))
            total = total + dot(jnp.concatenate(sides, 1), spread[256 * column : 256 * column + 256, :])
        return total

    def coarse_solve():
        upper_edge = 1.05 * bound[3]
        lower_edge = upper_edge / 20.0
        middle = 0.5 * (upper_edge + lower_edge)
        gap = 0.5 * (upper_edge - lower_edge)
        sigma = middle / gap
        left_half = iota((64, 128), 1) < 64
        halves = [slice(0, 64), slice(64, 128)]

        def send(parity, half, direction):
            high, rest = hi_lo(direction)
            coarse_own[parity, halves[half], :] = jnp.where(left_half, high, rest)
            begin(coarse_copies(parity, half))

        restrict()
        for half in range(2):
            direction = t_now[halves[half], :] / middle[0:1, :]
            send(0, half, direction)
            d_now[halves[half], :] = direction
            z_now[halves[half], :] = direction
        coarse_tables()

        def step(number, rho):
            parity = lax.rem(number, 2)
            rho_next = 1.0 / (2.0 * sigma - rho)
            for half in range(2):
                rows = halves[half]
                arrived(coarse_copies(parity, half))
                got = [coarse_own[parity, rows, :]] + [coarse_got[parity, k, rows, :] for k in range(4)]
                coupled = coarse_product(got)
                direction = d_now[rows, :]
                t_next = t_now[rows, :] - live[rows, :] * (cshift[rows, :] * direction + coarse_speed * coupled)
                t_now[rows, :] = t_next
                direction = (rho_next * rho)[0:1, :] * direction + (2.0 * rho_next / gap)[0:1, :] * t_next

                @pl.when(jnp.logical_and(number > 0, number < CHEB - 2))
                def _():
                    departed(coarse_copies(1 - parity, half))

                @pl.when(number < CHEB - 2)
                def _():
                    send(1 - parity, half, direction)

                d_now[rows, :] = direction
                z_now[rows, :] = z_now[rows, :] + direction
            return rho_next

        lax.fori_loop(0, CHEB - 1, step, 1.0 / sigma)
        for parity in range(2):
            for half in range(2):
                departed(coarse_copies(parity, half))

    def prolong(parity):
        following = 1 - parity
        slots = lax.shift_right_logical(iota((128, 128), 0) & 31, 2)
        half = lax.shift_right_logical(iota((128, 128), 1), 6)
        twice = jnp.concatenate([member_t[...], member_t[...]], 1)
        for pair in range(PAIRS):
            high, rest = hi_lo(jnp.where(slots == 2 * pair + half, z_now[...], 0.0))
            value = dot(twice, jnp.concatenate([high, rest], 0))
            field[pair] = field[pair] + value
            wide[following, pair + 1, EDGE : EDGE + ROWS, :] = value.astype(BF)

    field[...] = jnp.zeros(field.shape, F32)
    for pair in range(PAIRS):
        residual[pair] = rhs[pair]
        low[pair] = rhs[pair].astype(BF)

    def round_of(number, carry):
        parity = lax.rem(number, 2)

        @pl.when(number == 0)
        def _():
            for pair in range(PAIRS):
                load_smooth[pair].wait()
                relayout(raw_smooth, smoother, pair)

        @pl.when(number > 0)
        def _():
            operator_inner(parity)
            pl.when(number == 2)(member_table)
            scale = jnp.where(number == 3, 0.0, 1.0)
            operator_outer(parity, scale)
            halo_departed(parity)

        @pl.when(number == 2)
        def _():
            bound_end(2)
            coarse_solve()
            prolong(parity)
            for half in range(2):
                begin(stream_copies(1 - parity, half))
            span_begin(1 - parity)

        @pl.when(number != 2)
        def _():
            smooth_step(parity, number < 5)

        @pl.when(number == 0)
        def _():
            coarse_bound()
            bound_begin(0)
            for pair in range(PAIRS):
                load_diag[pair].wait()
                relayout(raw_diag, diag, pair)
            bound_end(0)
            bound_begin(1)

        @pl.when(number == 1)
        def _():
            bound_end(1)
            bound_begin(2)

        return carry

    lax.fori_loop(0, 6, round_of, 0)

    for pair in QUADS[1]:
        result_copy(pair).start()
    for pair in range(PAIRS):
        result_copy(pair).wait()


def unfold(field_hbm, out_hbm, field, out, load_sem, store_sem):
    loads = [pltpu.make_async_copy(field_hbm.at[pair], field.at[pair], load_sem.at[pair]) for pair in range(PAIRS)]
    stores = [
        pltpu.make_async_copy(out.at[pl.ds(2 * pair, 2)], out_hbm.at[pl.ds(2 * pair, 2)], store_sem.at[pair])
        for pair in range(PAIRS)
    ]
    for load in loads:
        load.start()
    for pair in range(PAIRS):
        loads[pair].wait()
        for vector in range(4):
            block = field[pair, pl.ds(vector, 128, stride=4), :].T
            out[2 * pair, vector] = block[0:64]
            out[2 * pair + 1, vector] = block[64:128]
        stores[pair].start()
    for store in stores:
        store.wait()


def local(stream_total, span_total, right_side, shift_fine, diag_blocks, smoother, couplings, coefficients,
          agg_ids, coarse_columns, coarse_blocks, coarse_shift):
    columns = jnp.transpose(coarse_columns, (0, 3, 1, 2))[0]
    blocks = jnp.transpose(coarse_blocks[0, 0], (1, 0, 2))
    vm = pltpu.VMEM
    dma = pltpu.SemaphoreType.DMA
    partners = (span_total - 1) + (min(8, stream_total) - 1) + (stream_total // min(8, stream_total) - 1)
    shape = (PAIRS, ROWS, 128)
    scratch = [
        vm((8, 4, 64, 128), F32), vm((8, 64, 128), F32), vm((8, 64, 64, 128), BF), vm((8, 64, 64, 128), BF),
        vm((8, 64, 64), BF), vm((8, 8, 128), F32), vm((8, 128), jnp.int32), vm((5, 1, 32), jnp.int32),
        vm((5, 32, 4096), F32), vm((32, 64), F32),
        vm((PAIRS, 8192, 128), BF), vm((PAIRS, 8192, 128), BF), vm(shape, F32), vm(shape, F32), vm(shape, F32),
        vm(shape, F32), vm(shape, F32), vm(shape, F32), vm(shape, BF), vm((2, PAIRS + 2, WROWS, 128), BF),
        vm((8,) + shape, BF), vm((1024, 128), BF),
        vm((128, 512), BF), vm((512, 128), BF), vm((4096, 128), BF), vm((5, 64, 64), BF), vm((128, 128), F32),
        vm((128, 128), F32), vm((128, 128), F32), vm((128, 128), F32), vm((128, 128), F32),
        vm((2, 128, 128), BF), vm((2, 4, 128, 128), BF),
        vm((4, 8, 128), F32), vm((partners, 8, 128), F32), vm((128, 128), BF), vm((128, 128), BF),
        dma((16,)), dma((2, 2, 2)), dma((2, 2, 2)), dma((2, 2)), dma((2, 2)), dma((2, 2, 4)), dma((2, 2, 4)), dma((partners,)), dma((partners,)), dma((4,)),
    ]
    anywhere = pl.BlockSpec(memory_space=pl.ANY)
    result = pl.pallas_call(
        functools.partial(kernel, stream_total, span_total),
        out_shape=jax.ShapeDtypeStruct(shape, F32),
        in_specs=[anywhere] * 10,
        out_specs=anywhere,
        scratch_shapes=scratch,
        compiler_params=pltpu.CompilerParams(
            collective_id=0, has_side_effects=True, vmem_limit_bytes=60 * 1024 * 1024
        ),
        name="cycle",
    )(right_side, shift_fine, diag_blocks, smoother, couplings, coefficients, agg_ids, columns, blocks,
      coarse_shift[0, 0])
    return pl.pallas_call(
        unfold,
        out_shape=jax.ShapeDtypeStruct(right_side.shape, F32),
        in_specs=[anywhere],
        out_specs=anywhere,
        scratch_shapes=[vm(shape, F32), vm((8, 4, 64, 128), F32), dma((PAIRS,)), dma((PAIRS,))],
        compiler_params=pltpu.CompilerParams(vmem_limit_bytes=60 * 1024 * 1024),
        name="unfold",
    )(result)


def solution(mesh):
    return jax.shard_map(
        functools.partial(local, mesh.shape["stream"], mesh.shape["span"]),
        mesh=mesh,
        in_specs=(
            P("stream", None, None, "span"),
            P("stream", None, "span"),
            P("stream", None, None, "span"),
            P("stream", None, None, "span"),
            P(),
            P(None, "stream", "span"),
            P("stream", "span"),
            P("stream", "span", None, None),
            P("stream", "span", None, None, None),
            P("stream", "span", None, None),
        ),
        out_specs=P("stream", None, None, "span"),
        check_vma=False,
    )
```

```python
import functools

import jax
import jax.numpy as jnp
from jax import lax
from jax.experimental import pallas as pl
from jax.experimental.pallas import tpu as pltpu
from jax.sharding import PartitionSpec as P

OMEGA = 0.3
CHEB = 8
BF = jnp.bfloat16
F32 = jnp.float32
MESH = pl.DeviceIdType.MESH
NT = (((1,), (1,)), ((), ()))
PAIRS = 4
QUADS = ((0, 3), (1, 2))
ROWS = 512
EDGE = 16
WROWS = ROWS + 2 * EDGE


def iota(shape, dim):
    return lax.broadcasted_iota(jnp.int32, shape, dim)


def one_zero(mask):
    return jnp.where(mask, 1.0, 0.0).astype(BF)


def dot(left, right):
    return jnp.dot(left, right, preferred_element_type=F32)


def dot_nt(left, right):
    return lax.dot_general(left, right, NT, preferred_element_type=F32)


def hi_lo(value):
    high = value.astype(BF)
    return high, (value - high.astype(F32)).astype(BF)


def block_tile(blocks, low, quad, step):
    left = iota((16, 128), 1) < 64
    node = lax.shift_right_logical(iota((16, 128), 0), 2)
    none = jnp.zeros((16, 128), BF)
    lines = []
    for value in low:
        other = pltpu.roll(value.astype(F32), 64, 1).astype(BF)
        for even, odd in ((value, other), (other, value)):
            halves = []
            for part in range(2):
                is_even = jnp.logical_and(node == 2 * part, left)
                is_odd = jnp.logical_and(node == 2 * part + 1, jnp.logical_not(left))
                halves.append(jnp.where(is_even, even, jnp.where(is_odd, odd, none)))
            lines.append(jnp.concatenate(halves, 1))
    rows = pl.ds(step * 256, 256)
    weights = jnp.concatenate([blocks[pair, rows, :] for pair in QUADS[quad]], 1)
    product = dot(jnp.concatenate(lines, 0), weights)
    results = []
    for half in range(2):
        columns = slice(128 * half, 128 * half + 128)
        first, second = product[32 * half : 32 * half + 16, columns], product[32 * half + 16 : 32 * half + 32, columns]
        results.append(jnp.where(left, first, second))
    return results


def relayout(raw, blocks, pair):
    def some_columns(group, carry):
        columns = pl.ds(pl.multiple_of(group * 16, 16), 16)
        cubes = []
        for half in range(2):
            for part in range(4):
                cube = jnp.stack([raw[2 * pair + half, 16 * part + a, columns, :] for a in range(16)], 0)
                cubes.append(jnp.transpose(cube, (1, 0, 2)))
        turned = [jnp.concatenate([cube[b] for cube in cubes], 0).T for b in range(16)]
        for part in range(8):
            cube = jnp.stack([one[16 * part : 16 * part + 16] for one in turned], 0)
            cube = jnp.transpose(cube, (1, 0, 2))
            for node in range(16):
                place = pl.multiple_of((part * 16 + node) * 64 + group * 16, 16)
                blocks[pair, pl.ds(place, 16), :] = cube[node]
        return carry

    lax.fori_loop(0, 4, some_columns, 0, unroll=2)


def kernel(
    stream_total,
    span_total,
    rhs_hbm, shift_hbm, diag_hbm, smooth_hbm, couple_hbm, coef_hbm, ids_hbm, cols_hbm, coarse_hbm, cshift_hbm,
    out_hbm,
    raw_rhs, raw_shift, raw_diag, raw_smooth, raw_couple, raw_coef, raw_ids, raw_cols, raw_coarse, raw_cshift,
    diag, smoother, rhs, shift, inverse, field, image, residual, low, wide, coef, couple,
    member, member_t, spread, pick, live, cshift, z_now, t_now, d_now, coarse_own, coarse_got,
    bound, bound_got, idpad, by_node,
    load_sem, halo_send, halo_recv, coarse_send, coarse_recv, bound_send, bound_recv, store_sem,
):
    position = lax.axis_index("stream")
    across = lax.axis_index("span")
    after = lax.rem(position + 1, stream_total)
    before = lax.rem(position + stream_total - 1, stream_total)
    right = lax.rem(across + 1, span_total)
    left = lax.rem(across + span_total - 1, span_total)
    group = min(8, stream_total)
    groups = stream_total // group

    stages = [[], [], []]
    for step in range(1, span_total):
        stages[0].append((position, lax.rem(across + step, span_total)))
    base = (position // group) * group
    for step in range(1, group):
        stages[1].append((base + lax.rem(position - base + step, group), across))
    for step in range(1, groups):
        stages[2].append((lax.rem(position + step * group, stream_total), across))
    partners = [who for stage in stages for who in stage]
    greeted = partners + [(after, across), (before, across)]

    @pl.when(position == 0)
    def _():
        for parity in range(2):
            wide[parity, 0] = jnp.zeros((WROWS, 128), BF)
            coarse_got[parity, 0] = jnp.zeros((128, 128), BF)

    @pl.when(position == stream_total - 1)
    def _():
        for parity in range(2):
            wide[parity, PAIRS + 1] = jnp.zeros((WROWS, 128), BF)
            coarse_got[parity, 1] = jnp.zeros((128, 128), BF)

    barrier = pltpu.get_barrier_semaphore()
    for who in greeted:
        pl.semaphore_signal(barrier, inc=1, device_id=who, device_id_type=MESH)

    loads = []

    def load(source, target):
        copy = pltpu.make_async_copy(source, target, load_sem.at[len(loads)])
        copy.start()
        loads.append(copy)
        return copy

    load_rhs = load(rhs_hbm, raw_rhs)
    load_shift = load(shift_hbm, raw_shift)
    load_ids = load(ids_hbm, raw_ids)
    load_cols = load(cols_hbm, raw_cols)
    load_cshift = load(cshift_hbm, raw_cshift)
    load_couple = load(couple_hbm, raw_couple)
    load_coef = load(coef_hbm, raw_coef)
    load_smooth = [
        load(smooth_hbm.at[pl.ds(2 * pair, 2)], raw_smooth.at[pl.ds(2 * pair, 2)]) for pair in range(PAIRS)
    ]
    load_coarse = load(coarse_hbm, raw_coarse)
    load_diag = [load(diag_hbm.at[pl.ds(2 * pair, 2)], raw_diag.at[pl.ds(2 * pair, 2)]) for pair in range(PAIRS)]

    def speed_of(place, extent):
        return jnp.sqrt(1.0 + 8.0 * (place + 0.5) / extent)

    here = position.astype(F32)
    coarse_speed = speed_of(jnp.full((1, 128), here, F32), float(stream_total))

    def spread_part(number, carry):
        rows = iota((128, 128), 0)
        lanes = iota((128, 128), 1)
        want = 2 * number + lax.shift_right_logical(rows, 6)
        spread[pl.ds(pl.multiple_of(number * 128, 128), 128), :] = one_zero((lanes & 63) == want)
        return carry

    lax.fori_loop(0, 32, spread_part, 0)

    load_rhs.wait()
    for pair in range(PAIRS):
        for vector in range(4):
            block = jnp.concatenate([raw_rhs[2 * pair, vector], raw_rhs[2 * pair + 1, vector]], 0)
            rhs[pair, pl.ds(vector, 128, stride=4), :] = block.T
    load_shift.wait()
    for pair in range(PAIRS):
        block = jnp.concatenate([raw_shift[2 * pair], raw_shift[2 * pair + 1]], 0).T
        for vector in range(4):
            shift[pair, pl.ds(vector, 128, stride=4), :] = block
        block = 1.0 / block
        for vector in range(4):
            inverse[pair, pl.ds(vector, 128, stride=4), :] = block

    load_ids.wait()
    idpad[...] = jnp.zeros(idpad.shape, BF)
    ids16 = jnp.concatenate([raw_ids[...].astype(F32), jnp.zeros((8, 128), F32)], 0).astype(BF)
    idpad[0:16, :] = ids16
    rows = iota((128, 128), 0)
    lanes = iota((128, 128), 1)
    expand = one_zero(lanes == lax.shift_right_logical(rows & 31, 2))
    by_slot = dot(expand, idpad[...])
    slot = (rows & 31).astype(F32)
    found = jnp.max(jnp.where(by_slot == slot, 1.0, 0.0), axis=1, keepdims=True)
    live[...] = jnp.broadcast_to(found, (128, 128))
    by_node[...] = by_slot.astype(BF)

    load_cshift.wait()
    twice = jnp.where((iota((64, 128), 1) & 63) == iota((64, 128), 0), 1.0, 0.0)
    doubled = jnp.dot(raw_cshift[...], twice, precision=lax.Precision.HIGHEST, preferred_element_type=F32)
    for vector in range(4):
        cshift[32 * vector : 32 * vector + 32, :] = doubled

    load_couple.wait()
    for number in range(8):
        one = raw_couple[number].astype(F32)
        none = jnp.zeros((64, 64), F32)
        both = jnp.concatenate([jnp.concatenate([one, none], 1), jnp.concatenate([none, one], 1)], 0)
        couple[number * 128 : number * 128 + 128, :] = both.T.astype(BF)

    load_coef.wait()
    rows = iota((512, 128), 0)
    lanes = iota((512, 128), 1)
    of_node = one_zero(lax.shift_right_logical(rows, 2) == lanes)
    place = iota((8, 128), 0)
    node_speed = speed_of(here * 8.0 + place.astype(F32), float(stream_total * 8))
    for number in range(8):
        weights = node_speed * raw_coef[number]
        for half in range(2):
            lines = jnp.concatenate(
                [jnp.broadcast_to(weights[4 * half + i : 4 * half + i + 1, :], (64, 128)) for i in range(4)], 0
            ).astype(BF)
            laid = dot_nt(of_node, lines).astype(BF)
            coef[number, 2 * half] = laid[:, :128]
            coef[number, 2 * half + 1] = laid[:, 128:]

    def member_table():
        rows = iota((128, 512), 0)
        lanes = iota((128, 512), 1)
        node_of = one_zero(lax.shift_right_logical(lanes, 2) == rows)
        wide_ids = dot(by_node[...], node_of)
        same = (lanes & 3) == lax.shift_right_logical(rows, 5)
        member[...] = one_zero(jnp.logical_and(wide_ids == (rows & 31).astype(F32), same))

    def coarse_tables():
        rows = iota((512, 128), 0)
        lanes = iota((512, 128), 1)
        of_node = one_zero(lax.shift_right_logical(rows, 2) == lanes)
        tall_ids = dot_nt(of_node, by_node[...])
        same = (rows & 3) == lax.shift_right_logical(lanes, 5)
        member_t[...] = one_zero(jnp.logical_and(tall_ids == (lanes & 31).astype(F32), same))

        load_cols.wait()
        repeat_rows = one_zero(iota((32, 32), 0) == iota((32, 32), 1))
        lanes = iota((32, 32), 1).astype(F32)
        for number in range(5):
            line = jnp.broadcast_to(raw_cols[number].astype(F32), (32, 32)).astype(BF)
            pick[number] = one_zero(dot_nt(repeat_rows, line) == lanes)

    pl.semaphore_wait(barrier, len(greeted))

    bound_copies = [
        pltpu.make_async_remote_copy(
            src_ref=bound.at[stage],
            dst_ref=bound_got.at[slot_number],
            send_sem=bound_send.at[slot_number],
            recv_sem=bound_recv.at[slot_number],
            device_id=who,
            device_id_type=MESH,
        )
        for slot_number, (stage, who) in enumerate(
            [(stage, who) for stage in range(3) for who in stages[stage]]
        )
    ]
    starts = [0, len(stages[0]), len(stages[0]) + len(stages[1]), len(partners)]

    def bound_begin(stage):
        for number in range(starts[stage], starts[stage + 1]):
            bound_copies[number].start()

    def bound_end(stage):
        value = bound[stage]
        for number in range(starts[stage], starts[stage + 1]):
            bound_copies[number].wait()
            value = jnp.maximum(value, bound_got[number])
        bound[stage + 1] = value

    def coarse_bound():
        load_coarse.wait()
        total = jnp.zeros((64, 128), F32)
        for number in range(32):
            columns = slice(128 * number, 128 * number + 128)
            size = jnp.abs(raw_coarse[0, :, columns])
            for kind in range(1, 5):
                size = size + jnp.abs(raw_coarse[kind, :, columns])
            high, rest = hi_lo(size)
            total = total + dot(jnp.concatenate([high, rest], 0), spread[columns, :])
        largest = live[0:32, :] * (cshift[0:32, :] + coarse_speed * (total[0:32] + total[32:64]))
        bound[0] = jnp.broadcast_to(jnp.max(jnp.max(largest, axis=1, keepdims=True), axis=0, keepdims=True), (8, 128))

    def begin(copies):
        for copy in copies[2:]:
            copy.start()
        pl.when(position < stream_total - 1)(copies[0].start)
        pl.when(position > 0)(copies[1].start)

    def arrived(copies):
        for copy in copies[2:]:
            copy.wait_recv()
        pl.when(position < stream_total - 1)(copies[1].wait_recv)
        pl.when(position > 0)(copies[0].wait_recv)

    def departed(copies):
        for copy in copies[2:]:
            copy.wait_send()
        pl.when(position < stream_total - 1)(copies[0].wait_send)
        pl.when(position > 0)(copies[1].wait_send)

    def halo_copy(source, target, send_sem, recv_sem, who):
        return pltpu.make_async_remote_copy(
            src_ref=source, dst_ref=target, send_sem=send_sem, recv_sem=recv_sem, device_id=who, device_id_type=MESH
        )

    def stream_copies(parity, first, start, size):
        mine = pl.ds(EDGE + start, size)
        ends = [(PAIRS, 0, after), (1, PAIRS + 1, before)]
        return [
            halo_copy(
                wide.at[parity, source, mine], wide.at[parity, target, mine],
                halo_send.at[parity, first + number], halo_recv.at[parity, first + number], (who, across),
            )
            for number, (source, target, who) in enumerate(ends)
        ]

    def span_copies(parity, first, low_pair, count):
        pairs = pl.ds(low_pair + 1, count)
        ends = [(ROWS, 0, right), (EDGE, ROWS + EDGE, left)]
        return [
            halo_copy(
                wide.at[parity, pairs, pl.ds(source, EDGE)], wide.at[parity, pairs, pl.ds(target, EDGE)],
                halo_send.at[parity, first + number], halo_recv.at[parity, first + number], (position, who),
            )
            for number, (source, target, who) in enumerate(ends)
        ]

    def middle_halo(parity):
        return [], span_copies(parity, 0, 1, 2)

    def edge_halo(parity):
        return (
            [stream_copies(parity, 2, 0, 128), stream_copies(parity, 4, 384, 128)],
            span_copies(parity, 6, 0, 1) + span_copies(parity, 8, 3, 1),
        )

    def core_halo(parity):
        return [stream_copies(parity, 10, 128, 256)], []

    def halo_begin(halo):
        for copies in halo[0]:
            begin(copies)
        for copy in halo[1]:
            copy.start()

    def halo_arrived(halo):
        for copies in halo[0]:
            arrived(copies)
        for copy in halo[1]:
            copy.wait_recv()

    def halo_departed(halo):
        for copies in halo[0]:
            departed(copies)
        for copy in halo[1]:
            copy.wait_send()

    def result_copy(pair):
        return pltpu.make_async_copy(field.at[pair], out_hbm.at[pair], store_sem.at[pair])

    def smooth_tiles(parity, quad, steps):
        following = 1 - parity
        for step in steps:
            rows = pl.ds(step * 16, 16)
            parts = block_tile(smoother, [low[pair, rows, :] for pair in QUADS[quad]], quad, step)
            for pair, part in zip(QUADS[quad], parts):
                change = residual[pair, rows, :] * inverse[pair, rows, :] + part
                value = field[pair, rows, :] + OMEGA * change
                field[pair, rows, :] = value
                wide[following, pair + 1, pl.ds(step * 16 + EDGE, 16), :] = value.astype(BF)

    def operator_inner(parity):
        for inside in range(64):
            quad, step = inside % 2, inside // 2
            rows = pl.ds(step * 16, 16)
            operand = [wide[parity, pair + 1, pl.ds(step * 16 + EDGE, 16), :] for pair in QUADS[quad]]
            parts = block_tile(diag, operand, quad, step)
            for pair, value, part in zip(QUADS[quad], operand, parts):
                image[pair, rows, :] = shift[pair, rows, :] * value.astype(F32) + part

    def stencil(parity, scale):
        def chunk(pair, start, size):
            left_half = iota((size, 128), 1) < 64
            rows = pl.ds(pl.multiple_of(start, 128), size)

            def at(which):
                return wide[parity, which, pl.ds(pl.multiple_of(start + EDGE, 16), size), :]

            here_now, lower, upper = at(pair + 1), at(pair), at(pair + 2)
            around = wide[parity, pair + 1, pl.ds(pl.multiple_of(start, 16), size + 2 * EDGE), :]
            shifted = [
                lower,
                pltpu.roll(jnp.where(left_half, here_now, lower).astype(F32), 64, 1).astype(BF),
                pltpu.roll(jnp.where(left_half, upper, here_now).astype(F32), 64, 1).astype(BF),
                upper,
                around[EDGE - 8 : EDGE - 8 + size],
                around[EDGE - 4 : EDGE - 4 + size],
                around[EDGE + 4 : EDGE + 4 + size],
                around[EDGE + 8 : EDGE + 8 + size],
            ]
            operand = jnp.concatenate([coef[m, pair, rows, :] * shifted[m] for m in range(8)], 1)
            value = scale * rhs[pair, rows, :] - (image[pair, rows, :] + dot(operand, couple[...]))
            residual[pair, rows, :] = value
            low[pair, rows, :] = value.astype(BF)

        return chunk

    def coarse_copies(parity, vector):
        targets = [(after, across), (before, across), (position, right), (position, left)]
        rows = pl.ds(32 * vector, 32)
        return [
            pltpu.make_async_remote_copy(
                src_ref=coarse_own.at[parity, rows],
                dst_ref=coarse_got.at[parity, number, rows],
                send_sem=coarse_send.at[parity, vector, number],
                recv_sem=coarse_recv.at[parity, vector, number],
                device_id=who,
                device_id_type=MESH,
            )
            for number, who in enumerate(targets)
        ]

    def restrict():
        total = jnp.zeros((128, 512), F32)
        parts = []
        for pair in range(PAIRS):
            high, rest = hi_lo(residual[pair])
            parts.append(dot(member[...], high) + dot(member[...], rest))
        left_half = iota((8, 128), 1) < 64
        top = iota((8, 128), 0) < 4
        for vector in range(4):
            for pair in range(PAIRS):
                begin = 32 * vector + 8 * pair
                own = jnp.where(top == left_half, parts[pair][begin : begin + 8, :], 0.0)
                t_now[begin : begin + 8, :] = own + pltpu.roll(own, 64, 1)

    def coarse_product(got):
        near = []
        for number in range(5):
            value = dot(pick[number], got[number])
            near.append(value + pltpu.roll(value, 64, 1))
        total = jnp.zeros((32, 128), F32)
        for column in range(16):
            sides = []
            for side in range(2):
                begin_at = 256 * column + 128 * side
                blocks = [raw_coarse[k, :, begin_at : begin_at + 128] for k in range(5)]
                part = blocks[0] * near[0]
                for k in range(1, 5):
                    part = part + blocks[k] * near[k]
                sides.append(part.astype(BF))
            total = total + dot(jnp.concatenate(sides, 1), spread[256 * column : 256 * column + 256, :])
        return total

    def coarse_solve():
        upper_edge = 1.05 * bound[3]
        lower_edge = upper_edge / 20.0
        middle = 0.5 * (upper_edge + lower_edge)
        gap = 0.5 * (upper_edge - lower_edge)
        sigma = middle / gap
        left_half = iota((32, 128), 1) < 64
        vectors = [slice(32 * vector, 32 * vector + 32) for vector in range(4)]

        def send(parity, vector, direction):
            high, rest = hi_lo(direction)
            coarse_own[parity, vectors[vector], :] = jnp.where(left_half, high, rest)
            begin(coarse_copies(parity, vector))

        restrict()
        for vector in range(4):
            direction = t_now[vectors[vector], :] / middle[0:1, :]
            send(0, vector, direction)
            d_now[vectors[vector], :] = direction
            z_now[vectors[vector], :] = direction
        coarse_tables()

        def step(number, rho):
            parity = lax.rem(number, 2)
            rho_next = 1.0 / (2.0 * sigma - rho)
            for vector in range(4):
                rows = vectors[vector]
                arrived(coarse_copies(parity, vector))
                got = [coarse_own[parity, rows, :]] + [coarse_got[parity, k, rows, :] for k in range(4)]
                coupled = coarse_product(got)
                direction = d_now[rows, :]
                t_next = t_now[rows, :] - live[rows, :] * (cshift[rows, :] * direction + coarse_speed * coupled)
                t_now[rows, :] = t_next
                direction = (rho_next * rho)[0:1, :] * direction + (2.0 * rho_next / gap)[0:1, :] * t_next

                @pl.when(jnp.logical_and(number > 0, number < CHEB - 2))
                def _():
                    departed(coarse_copies(1 - parity, vector))

                @pl.when(number < CHEB - 2)
                def _():
                    send(1 - parity, vector, direction)

                d_now[rows, :] = direction
                z_now[rows, :] = z_now[rows, :] + direction
            return rho_next

        lax.fori_loop(0, CHEB - 1, step, 1.0 / sigma)
        for parity in range(2):
            for vector in range(4):
                departed(coarse_copies(parity, vector))

    def prolong(parity):
        following = 1 - parity
        slots = lax.shift_right_logical(iota((128, 128), 0) & 31, 2)
        half = lax.shift_right_logical(iota((128, 128), 1), 6)
        twice = jnp.concatenate([member_t[...], member_t[...]], 1)
        for pair in range(PAIRS):
            high, rest = hi_lo(jnp.where(slots == 2 * pair + half, z_now[...], 0.0))
            value = dot(twice, jnp.concatenate([high, rest], 0))
            field[pair] = field[pair] + value
            wide[following, pair + 1, EDGE : EDGE + ROWS, :] = value.astype(BF)

    field[...] = jnp.zeros(field.shape, F32)
    for pair in range(PAIRS):
        residual[pair] = rhs[pair]
        low[pair] = rhs[pair].astype(BF)

    def round_of(number, carry):
        parity = lax.rem(number, 2)

        @pl.when(number == 0)
        def _():
            for pair in range(PAIRS):
                load_smooth[pair].wait()
                relayout(raw_smooth, smoother, pair)

        following = 1 - parity
        more = number < 5
        chunk = stencil(parity, jnp.where(number == 3, 0.0, 1.0))
        ends = (0, 384)

        @pl.when(number > 0)
        def _():
            operator_inner(parity)
            pl.when(number == 2)(member_table)
            for pair in QUADS[1]:
                chunk(pair, 128, 256)
            halo_arrived(middle_halo(parity))
            for pair in QUADS[1]:
                for start in ends:
                    chunk(pair, start, 128)

        @pl.when(number != 2)
        def _():
            smooth_tiles(parity, 1, (0, 31))
            pl.when(more)(lambda: halo_begin(middle_halo(following)))

        @pl.when(number > 0)
        def _():
            halo_arrived(edge_halo(parity))
            for pair in QUADS[0]:
                for start in ends:
                    chunk(pair, start, 128)

        @pl.when(number != 2)
        def _():
            smooth_tiles(parity, 0, [*range(8), *range(24, 32)])
            pl.when(more)(lambda: halo_begin(edge_halo(following)))

        @pl.when(number > 0)
        def _():
            halo_arrived(core_halo(parity))
            for pair in QUADS[0]:
                chunk(pair, 128, 256)

        @pl.when(number != 2)
        def _():
            smooth_tiles(parity, 0, range(8, 24))
            pl.when(more)(lambda: halo_begin(core_halo(following)))

        @pl.when(number == 2)
        def _():
            bound_end(2)
            coarse_solve()
            prolong(parity)
            for halo in (middle_halo, edge_halo, core_halo):
                halo_begin(halo(following))

        @pl.when(number == 5)
        def _():
            for pair in QUADS[0]:
                result_copy(pair).start()

        @pl.when(number != 2)
        def _():
            smooth_tiles(parity, 1, range(1, 31))

        @pl.when(number > 0)
        def _():
            for halo in (middle_halo, edge_halo, core_halo):
                halo_departed(halo(parity))

        @pl.when(number == 0)
        def _():
            coarse_bound()
            bound_begin(0)
            for pair in range(PAIRS):
                load_diag[pair].wait()
                relayout(raw_diag, diag, pair)
            bound_end(0)
            bound_begin(1)

        @pl.when(number == 1)
        def _():
            bound_end(1)
            bound_begin(2)

        return carry

    lax.fori_loop(0, 6, round_of, 0)

    for pair in QUADS[1]:
        result_copy(pair).start()
    for pair in range(PAIRS):
        result_copy(pair).wait()


def unfold(field_hbm, out_hbm, field, out, load_sem, store_sem):
    loads = [pltpu.make_async_copy(field_hbm.at[pair], field.at[pair], load_sem.at[pair]) for pair in range(PAIRS)]
    stores = [
        pltpu.make_async_copy(out.at[pl.ds(2 * pair, 2)], out_hbm.at[pl.ds(2 * pair, 2)], store_sem.at[pair])
        for pair in range(PAIRS)
    ]
    for load in loads:
        load.start()
    for pair in range(PAIRS):
        loads[pair].wait()
        for vector in range(4):
            block = field[pair, pl.ds(vector, 128, stride=4), :].T
            out[2 * pair, vector] = block[0:64]
            out[2 * pair + 1, vector] = block[64:128]
        stores[pair].start()
    for store in stores:
        store.wait()


def local(stream_total, span_total, right_side, shift_fine, diag_blocks, smoother, couplings, coefficients,
          agg_ids, coarse_columns, coarse_blocks, coarse_shift):
    columns = jnp.transpose(coarse_columns, (0, 3, 1, 2))[0]
    blocks = jnp.transpose(coarse_blocks[0, 0], (1, 0, 2))
    vm = pltpu.VMEM
    dma = pltpu.SemaphoreType.DMA
    partners = (span_total - 1) + (min(8, stream_total) - 1) + (stream_total // min(8, stream_total) - 1)
    shape = (PAIRS, ROWS, 128)
    scratch = [
        vm((8, 4, 64, 128), F32), vm((8, 64, 128), F32), vm((8, 64, 64, 128), BF), vm((8, 64, 64, 128), BF),
        vm((8, 64, 64), BF), vm((8, 8, 128), F32), vm((8, 128), jnp.int32), vm((5, 1, 32), jnp.int32),
        vm((5, 32, 4096), F32), vm((32, 64), F32),
        vm((PAIRS, 8192, 128), BF), vm((PAIRS, 8192, 128), BF), vm(shape, F32), vm(shape, F32), vm(shape, F32),
        vm(shape, F32), vm(shape, F32), vm(shape, F32), vm(shape, BF), vm((2, PAIRS + 2, WROWS, 128), BF),
        vm((8,) + shape, BF), vm((1024, 128), BF),
        vm((128, 512), BF), vm((512, 128), BF), vm((4096, 128), BF), vm((5, 32, 32), BF), vm((128, 128), F32),
        vm((128, 128), F32), vm((128, 128), F32), vm((128, 128), F32), vm((128, 128), F32),
        vm((2, 128, 128), BF), vm((2, 4, 128, 128), BF),
        vm((4, 8, 128), F32), vm((partners, 8, 128), F32), vm((128, 128), BF), vm((128, 128), BF),
        dma((16,)), dma((2, 12)), dma((2, 12)), dma((2, 4, 4)), dma((2, 4, 4)), dma((partners,)), dma((partners,)), dma((4,)),
    ]
    anywhere = pl.BlockSpec(memory_space=pl.ANY)
    result = pl.pallas_call(
        functools.partial(kernel, stream_total, span_total),
        out_shape=jax.ShapeDtypeStruct(shape, F32),
        in_specs=[anywhere] * 10,
        out_specs=anywhere,
        scratch_shapes=scratch,
        compiler_params=pltpu.CompilerParams(
            collective_id=0, has_side_effects=True, vmem_limit_bytes=60 * 1024 * 1024
        ),
        name="cycle",
    )(right_side, shift_fine, diag_blocks, smoother, couplings, coefficients, agg_ids, columns, blocks,
      coarse_shift[0, 0])
    return pl.pallas_call(
        unfold,
        out_shape=jax.ShapeDtypeStruct(right_side.shape, F32),
        in_specs=[anywhere],
        out_specs=anywhere,
        scratch_shapes=[vm(shape, F32), vm((8, 4, 64, 128), F32), dma((PAIRS,)), dma((PAIRS,))],
        compiler_params=pltpu.CompilerParams(vmem_limit_bytes=60 * 1024 * 1024),
        name="unfold",
    )(result)


def solution(mesh):
    return jax.shard_map(
        functools.partial(local, mesh.shape["stream"], mesh.shape["span"]),
        mesh=mesh,
        in_specs=(
            P("stream", None, None, "span"),
            P("stream", None, "span"),
            P("stream", None, None, "span"),
            P("stream", None, None, "span"),
            P(),
            P(None, "stream", "span"),
            P("stream", "span"),
            P("stream", "span", None, None),
            P("stream", "span", None, None, None),
            P("stream", "span", None, None),
        ),
        out_specs=P("stream", None, None, "span"),
        check_vma=False,
    )
```

```python
import functools

import jax
import jax.numpy as jnp
from jax import lax
from jax.experimental import pallas as pl
from jax.experimental.pallas import tpu as pltpu
from jax.sharding import PartitionSpec as P

OMEGA = 0.3
CHEB = 8
BF = jnp.bfloat16
F32 = jnp.float32
MESH = pl.DeviceIdType.MESH
NT = (((1,), (1,)), ((), ()))
PAIRS = 4
QUADS = ((0, 3), (1, 2))
ROWS = 512
EDGE = 16
WROWS = ROWS + 2 * EDGE


def iota(shape, dim):
    return lax.broadcasted_iota(jnp.int32, shape, dim)


def one_zero(mask):
    return jnp.where(mask, 1.0, 0.0).astype(BF)


def dot(left, right):
    return jnp.dot(left, right, preferred_element_type=F32)


def dot_nt(left, right):
    return lax.dot_general(left, right, NT, preferred_element_type=F32)


def hi_lo(value):
    high = value.astype(BF)
    return high, (value - high.astype(F32)).astype(BF)


def block_tile(blocks, low, quad, step):
    left = iota((16, 128), 1) < 64
    node = lax.shift_right_logical(iota((16, 128), 0), 2)
    none = jnp.zeros((16, 128), BF)
    lines = []
    for value in low:
        other = pltpu.roll(value.astype(F32), 64, 1).astype(BF)
        for even, odd in ((value, other), (other, value)):
            halves = []
            for part in range(2):
                is_even = jnp.logical_and(node == 2 * part, left)
                is_odd = jnp.logical_and(node == 2 * part + 1, jnp.logical_not(left))
                halves.append(jnp.where(is_even, even, jnp.where(is_odd, odd, none)))
            lines.append(jnp.concatenate(halves, 1))
    rows = pl.ds(step * 256, 256)
    weights = jnp.concatenate([blocks[pair, rows, :] for pair in QUADS[quad]], 1)
    product = dot(jnp.concatenate(lines, 0), weights)
    results = []
    for half in range(2):
        columns = slice(128 * half, 128 * half + 128)
        first, second = product[32 * half : 32 * half + 16, columns], product[32 * half + 16 : 32 * half + 32, columns]
        results.append(jnp.where(left, first, second))
    return results


def relayout(raw, blocks, pair):
    def some_columns(group, carry):
        columns = pl.ds(pl.multiple_of(group * 16, 16), 16)
        cubes = []
        for half in range(2):
            for part in range(4):
                cube = jnp.stack([raw[2 * pair + half, 16 * part + a, columns, :] for a in range(16)], 0)
                cubes.append(jnp.transpose(cube, (1, 0, 2)))
        turned = [jnp.concatenate([cube[b] for cube in cubes], 0).T for b in range(16)]
        for part in range(8):
            cube = jnp.stack([one[16 * part : 16 * part + 16] for one in turned], 0)
            cube = jnp.transpose(cube, (1, 0, 2))
            for node in range(16):
                place = pl.multiple_of((part * 16 + node) * 64 + group * 16, 16)
                blocks[pair, pl.ds(place, 16), :] = cube[node]
        return carry

    lax.fori_loop(0, 4, some_columns, 0, unroll=4)


def kernel(
    stream_total,
    span_total,
    rhs_hbm, shift_hbm, diag_hbm, smooth_hbm, couple_hbm, coef_hbm, ids_hbm, cols_hbm, coarse_hbm, cshift_hbm,
    out_hbm,
    raw_rhs, raw_shift, raw_diag, raw_smooth, raw_couple, raw_coef, raw_ids, raw_cols, raw_coarse, raw_cshift,
    diag, smoother, rhs, shift, inverse, field, image, residual, low, wide, coef, couple,
    member, member_t, spread, pick, live, cshift, z_now, t_now, d_now, coarse_own, coarse_got,
    bound, bound_got, idpad, by_node,
    load_sem, halo_send, halo_recv, coarse_send, coarse_recv, bound_send, bound_recv, store_sem,
):
    position = lax.axis_index("stream")
    across = lax.axis_index("span")
    after = lax.rem(position + 1, stream_total)
    before = lax.rem(position + stream_total - 1, stream_total)
    right = lax.rem(across + 1, span_total)
    left = lax.rem(across + span_total - 1, span_total)
    group = min(8, stream_total)
    groups = stream_total // group

    stages = [[], [], []]
    for step in range(1, span_total):
        stages[0].append((position, lax.rem(across + step, span_total)))
    base = (position // group) * group
    for step in range(1, group):
        stages[1].append((base + lax.rem(position - base + step, group), across))
    for step in range(1, groups):
        stages[2].append((lax.rem(position + step * group, stream_total), across))
    partners = [who for stage in stages for who in stage]
    greeted = partners + [(after, across), (before, across)]

    loads = []

    def load(source, target):
        copy = pltpu.make_async_copy(source, target, load_sem.at[len(loads)])
        copy.start()
        loads.append(copy)
        return copy

    load_rhs = load(rhs_hbm, raw_rhs)
    load_shift = load(shift_hbm, raw_shift)
    load_ids = load(ids_hbm, raw_ids)
    load_cols = load(cols_hbm, raw_cols)
    load_cshift = load(cshift_hbm, raw_cshift)
    load_couple = load(couple_hbm, raw_couple)
    load_coef = load(coef_hbm, raw_coef)
    load_smooth = [
        load(smooth_hbm.at[pl.ds(2 * pair, 2)], raw_smooth.at[pl.ds(2 * pair, 2)]) for pair in range(PAIRS)
    ]
    load_coarse = load(coarse_hbm, raw_coarse)
    load_diag = [load(diag_hbm.at[pl.ds(2 * pair, 2)], raw_diag.at[pl.ds(2 * pair, 2)]) for pair in range(PAIRS)]

    @pl.when(position == 0)
    def _():
        for parity in range(2):
            wide[parity, 0] = jnp.zeros((WROWS, 128), BF)
            coarse_got[parity, 0] = jnp.zeros((128, 128), BF)

    @pl.when(position == stream_total - 1)
    def _():
        for parity in range(2):
            wide[parity, PAIRS + 1] = jnp.zeros((WROWS, 128), BF)
            coarse_got[parity, 1] = jnp.zeros((128, 128), BF)

    barrier = pltpu.get_barrier_semaphore()
    for who in greeted:
        pl.semaphore_signal(barrier, inc=1, device_id=who, device_id_type=MESH)

    def speed_of(place, extent):
        return jnp.sqrt(1.0 + 8.0 * (place + 0.5) / extent)

    here = position.astype(F32)
    coarse_speed = speed_of(jnp.full((1, 128), here, F32), float(stream_total))

    def spread_part(number, carry):
        rows = iota((128, 128), 0)
        lanes = iota((128, 128), 1)
        want = 2 * number + lax.shift_right_logical(rows, 6)
        spread[pl.ds(pl.multiple_of(number * 128, 128), 128), :] = one_zero((lanes & 63) == want)
        return carry

    lax.fori_loop(0, 32, spread_part, 0)

    load_rhs.wait()
    for pair in range(PAIRS):
        for vector in range(4):
            block = jnp.concatenate([raw_rhs[2 * pair, vector], raw_rhs[2 * pair + 1, vector]], 0)
            rhs[pair, pl.ds(vector, 128, stride=4), :] = block.T
    load_shift.wait()
    for pair in range(PAIRS):
        block = jnp.concatenate([raw_shift[2 * pair], raw_shift[2 * pair + 1]], 0).T
        for vector in range(4):
            shift[pair, pl.ds(vector, 128, stride=4), :] = block
        block = 1.0 / block
        for vector in range(4):
            inverse[pair, pl.ds(vector, 128, stride=4), :] = block

    load_ids.wait()
    idpad[...] = jnp.zeros(idpad.shape, BF)
    ids16 = jnp.concatenate([raw_ids[...].astype(F32), jnp.zeros((8, 128), F32)], 0).astype(BF)
    idpad[0:16, :] = ids16
    rows = iota((128, 128), 0)
    lanes = iota((128, 128), 1)
    expand = one_zero(lanes == lax.shift_right_logical(rows & 31, 2))
    by_slot = dot(expand, idpad[...])
    slot = (rows & 31).astype(F32)
    found = jnp.max(jnp.where(by_slot == slot, 1.0, 0.0), axis=1, keepdims=True)
    live[...] = jnp.broadcast_to(found, (128, 128))
    by_node[...] = by_slot.astype(BF)

    load_cshift.wait()
    twice = jnp.where((iota((64, 128), 1) & 63) == iota((64, 128), 0), 1.0, 0.0)
    doubled = jnp.dot(raw_cshift[...], twice, precision=lax.Precision.HIGHEST, preferred_element_type=F32)
    for vector in range(4):
        cshift[32 * vector : 32 * vector + 32, :] = doubled

    load_couple.wait()
    for number in range(8):
        one = raw_couple[number].astype(F32)
        none = jnp.zeros((64, 64), F32)
        both = jnp.concatenate([jnp.concatenate([one, none], 1), jnp.concatenate([none, one], 1)], 0)
        couple[number * 128 : number * 128 + 128, :] = both.T.astype(BF)

    load_coef.wait()
    rows = iota((512, 128), 0)
    lanes = iota((512, 128), 1)
    of_node = one_zero(lax.shift_right_logical(rows, 2) == lanes)
    place = iota((8, 128), 0)
    node_speed = speed_of(here * 8.0 + place.astype(F32), float(stream_total * 8))
    for number in range(8):
        weights = node_speed * raw_coef[number]
        for half in range(2):
            lines = jnp.concatenate(
                [jnp.broadcast_to(weights[4 * half + i : 4 * half + i + 1, :], (64, 128)) for i in range(4)], 0
            ).astype(BF)
            laid = dot_nt(of_node, lines).astype(BF)
            coef[number, 2 * half] = laid[:, :128]
            coef[number, 2 * half + 1] = laid[:, 128:]

    def member_table():
        rows = iota((128, 512), 0)
        lanes = iota((128, 512), 1)
        node_of = one_zero(lax.shift_right_logical(lanes, 2) == rows)
        wide_ids = dot(by_node[...], node_of)
        same = (lanes & 3) == lax.shift_right_logical(rows, 5)
        member[...] = one_zero(jnp.logical_and(wide_ids == (rows & 31).astype(F32), same))

    def coarse_tables():
        rows = iota((512, 128), 0)
        lanes = iota((512, 128), 1)
        of_node = one_zero(lax.shift_right_logical(rows, 2) == lanes)
        tall_ids = dot_nt(of_node, by_node[...])
        same = (rows & 3) == lax.shift_right_logical(lanes, 5)
        member_t[...] = one_zero(jnp.logical_and(tall_ids == (lanes & 31).astype(F32), same))

        load_cols.wait()
        repeat_rows = one_zero(iota((32, 32), 0) == iota((32, 32), 1))
        lanes = iota((32, 32), 1).astype(F32)
        for number in range(5):
            line = jnp.broadcast_to(raw_cols[number].astype(F32), (32, 32)).astype(BF)
            pick[number] = one_zero(dot_nt(repeat_rows, line) == lanes)

    pl.semaphore_wait(barrier, len(greeted))

    bound_copies = [
        pltpu.make_async_remote_copy(
            src_ref=bound.at[stage],
            dst_ref=bound_got.at[slot_number],
            send_sem=bound_send.at[slot_number],
            recv_sem=bound_recv.at[slot_number],
            device_id=who,
            device_id_type=MESH,
        )
        for slot_number, (stage, who) in enumerate(
            [(stage, who) for stage in range(3) for who in stages[stage]]
        )
    ]
    starts = [0, len(stages[0]), len(stages[0]) + len(stages[1]), len(partners)]

    def bound_begin(stage):
        for number in range(starts[stage], starts[stage + 1]):
            bound_copies[number].start()

    def bound_end(stage):
        value = bound[stage]
        for number in range(starts[stage], starts[stage + 1]):
            bound_copies[number].wait()
            value = jnp.maximum(value, bound_got[number])
        bound[stage + 1] = value

    def coarse_bound():
        load_coarse.wait()
        total = jnp.zeros((64, 128), F32)
        for number in range(32):
            columns = slice(128 * number, 128 * number + 128)
            size = jnp.abs(raw_coarse[0, :, columns])
            for kind in range(1, 5):
                size = size + jnp.abs(raw_coarse[kind, :, columns])
            high, rest = hi_lo(size)
            total = total + dot(jnp.concatenate([high, rest], 0), spread[columns, :])
        largest = live[0:32, :] * (cshift[0:32, :] + coarse_speed * (total[0:32] + total[32:64]))
        bound[0] = jnp.broadcast_to(jnp.max(jnp.max(largest, axis=1, keepdims=True), axis=0, keepdims=True), (8, 128))

    def begin(copies):
        for copy in copies[2:]:
            copy.start()
        pl.when(position < stream_total - 1)(copies[0].start)
        pl.when(position > 0)(copies[1].start)

    def arrived(copies):
        for copy in copies[2:]:
            copy.wait_recv()
        pl.when(position < stream_total - 1)(copies[1].wait_recv)
        pl.when(position > 0)(copies[0].wait_recv)

    def departed(copies):
        for copy in copies[2:]:
            copy.wait_send()
        pl.when(position < stream_total - 1)(copies[0].wait_send)
        pl.when(position > 0)(copies[1].wait_send)

    def halo_copy(source, target, send_sem, recv_sem, who):
        return pltpu.make_async_remote_copy(
            src_ref=source, dst_ref=target, send_sem=send_sem, recv_sem=recv_sem, device_id=who, device_id_type=MESH
        )

    def stream_copies(parity, first, start, size):
        mine = pl.ds(EDGE + start, size)
        ends = [(PAIRS, 0, after), (1, PAIRS + 1, before)]
        return [
            halo_copy(
                wide.at[parity, source, mine], wide.at[parity, target, mine],
                halo_send.at[parity, first + number], halo_recv.at[parity, first + number], (who, across),
            )
            for number, (source, target, who) in enumerate(ends)
        ]

    def span_copies(parity, first, low_pair, count):
        pairs = pl.ds(low_pair + 1, count)
        ends = [(ROWS, 0, right), (EDGE, ROWS + EDGE, left)]
        return [
            halo_copy(
                wide.at[parity, pairs, pl.ds(source, EDGE)], wide.at[parity, pairs, pl.ds(target, EDGE)],
                halo_send.at[parity, first + number], halo_recv.at[parity, first + number], (position, who),
            )
            for number, (source, target, who) in enumerate(ends)
        ]

    def middle_halo(parity):
        return [], span_copies(parity, 0, 1, 2)

    def edge_halo(parity):
        return (
            [stream_copies(parity, 2, 0, 128), stream_copies(parity, 4, 384, 128)],
            span_copies(parity, 6, 0, 1) + span_copies(parity, 8, 3, 1),
        )

    def core_halo(parity):
        return [stream_copies(parity, 10, 128, 256)], []

    def halo_begin(halo):
        for copies in halo[0]:
            begin(copies)
        for copy in halo[1]:
            copy.start()

    def halo_arrived(halo):
        for copies in halo[0]:
            arrived(copies)
        for copy in halo[1]:
            copy.wait_recv()

    def halo_departed(halo):
        for copies in halo[0]:
            departed(copies)
        for copy in halo[1]:
            copy.wait_send()

    def result_copy(pair):
        return pltpu.make_async_copy(field.at[pair], out_hbm.at[pair], store_sem.at[pair])

    def smooth_tiles(parity, quad, steps):
        following = 1 - parity
        for step in steps:
            rows = pl.ds(step * 16, 16)
            parts = block_tile(smoother, [low[pair, rows, :] for pair in QUADS[quad]], quad, step)
            for pair, part in zip(QUADS[quad], parts):
                change = residual[pair, rows, :] * inverse[pair, rows, :] + part
                value = field[pair, rows, :] + OMEGA * change
                field[pair, rows, :] = value
                wide[following, pair + 1, pl.ds(step * 16 + EDGE, 16), :] = value.astype(BF)

    def operator_inner(parity):
        for inside in range(64):
            quad, step = inside % 2, inside // 2
            rows = pl.ds(step * 16, 16)
            operand = [wide[parity, pair + 1, pl.ds(step * 16 + EDGE, 16), :] for pair in QUADS[quad]]
            parts = block_tile(diag, operand, quad, step)
            for pair, value, part in zip(QUADS[quad], operand, parts):
                image[pair, rows, :] = shift[pair, rows, :] * value.astype(F32) + part

    def stencil(parity, scale):
        def chunk(pair, start, size):
            left_half = iota((size, 128), 1) < 64
            rows = pl.ds(pl.multiple_of(start, 128), size)

            def at(which):
                return wide[parity, which, pl.ds(pl.multiple_of(start + EDGE, 16), size), :]

            here_now, lower, upper = at(pair + 1), at(pair), at(pair + 2)
            around = wide[parity, pair + 1, pl.ds(pl.multiple_of(start, 16), size + 2 * EDGE), :]
            shifted = [
                lower,
                pltpu.roll(jnp.where(left_half, here_now, lower).astype(F32), 64, 1).astype(BF),
                pltpu.roll(jnp.where(left_half, upper, here_now).astype(F32), 64, 1).astype(BF),
                upper,
                around[EDGE - 8 : EDGE - 8 + size],
                around[EDGE - 4 : EDGE - 4 + size],
                around[EDGE + 4 : EDGE + 4 + size],
                around[EDGE + 8 : EDGE + 8 + size],
            ]
            operand = jnp.concatenate([coef[m, pair, rows, :] * shifted[m] for m in range(8)], 1)
            value = scale * rhs[pair, rows, :] - (image[pair, rows, :] + dot(operand, couple[...]))
            residual[pair, rows, :] = value
            low[pair, rows, :] = value.astype(BF)

        return chunk

    def coarse_copies(parity, vector):
        targets = [(after, across), (before, across), (position, right), (position, left)]
        rows = pl.ds(32 * vector, 32)
        return [
            pltpu.make_async_remote_copy(
                src_ref=coarse_own.at[parity, rows],
                dst_ref=coarse_got.at[parity, number, rows],
                send_sem=coarse_send.at[parity, vector, number],
                recv_sem=coarse_recv.at[parity, vector, number],
                device_id=who,
                device_id_type=MESH,
            )
            for number, who in enumerate(targets)
        ]

    def restrict():
        total = jnp.zeros((128, 512), F32)
        parts = []
        for pair in range(PAIRS):
            high, rest = hi_lo(residual[pair])
            parts.append(dot(member[...], high) + dot(member[...], rest))
        left_half = iota((8, 128), 1) < 64
        top = iota((8, 128), 0) < 4
        for vector in range(4):
            for pair in range(PAIRS):
                begin = 32 * vector + 8 * pair
                own = jnp.where(top == left_half, parts[pair][begin : begin + 8, :], 0.0)
                t_now[begin : begin + 8, :] = own + pltpu.roll(own, 64, 1)

    def coarse_product(got):
        near = []
        for number in range(5):
            value = dot(pick[number], got[number])
            near.append(value + pltpu.roll(value, 64, 1))
        total = jnp.zeros((32, 128), F32)
        for column in range(16):
            sides = []
            for side in range(2):
                begin_at = 256 * column + 128 * side
                blocks = [raw_coarse[k, :, begin_at : begin_at + 128] for k in range(5)]
                part = blocks[0] * near[0]
                for k in range(1, 5):
                    part = part + blocks[k] * near[k]
                sides.append(part.astype(BF))
            total = total + dot(jnp.concatenate(sides, 1), spread[256 * column : 256 * column + 256, :])
        return total

    def coarse_solve():
        upper_edge = 1.05 * bound[3]
        lower_edge = upper_edge / 20.0
        middle = 0.5 * (upper_edge + lower_edge)
        gap = 0.5 * (upper_edge - lower_edge)
        sigma = middle / gap
        left_half = iota((32, 128), 1) < 64
        vectors = [slice(32 * vector, 32 * vector + 32) for vector in range(4)]

        def send(parity, vector, direction):
            high, rest = hi_lo(direction)
            coarse_own[parity, vectors[vector], :] = jnp.where(left_half, high, rest)
            begin(coarse_copies(parity, vector))

        restrict()
        for vector in range(4):
            direction = t_now[vectors[vector], :] / middle[0:1, :]
            send(0, vector, direction)
            d_now[vectors[vector], :] = direction
            z_now[vectors[vector], :] = direction
        coarse_tables()

        def step(number, rho):
            parity = lax.rem(number, 2)
            rho_next = 1.0 / (2.0 * sigma - rho)
            for vector in range(4):
                rows = vectors[vector]
                arrived(coarse_copies(parity, vector))
                got = [coarse_own[parity, rows, :]] + [coarse_got[parity, k, rows, :] for k in range(4)]
                coupled = coarse_product(got)
                direction = d_now[rows, :]
                t_next = t_now[rows, :] - live[rows, :] * (cshift[rows, :] * direction + coarse_speed * coupled)
                t_now[rows, :] = t_next
                direction = (rho_next * rho)[0:1, :] * direction + (2.0 * rho_next / gap)[0:1, :] * t_next

                @pl.when(jnp.logical_and(number > 0, number < CHEB - 2))
                def _():
                    departed(coarse_copies(1 - parity, vector))

                @pl.when(number < CHEB - 2)
                def _():
                    send(1 - parity, vector, direction)

                d_now[rows, :] = direction
                z_now[rows, :] = z_now[rows, :] + direction
            return rho_next

        lax.fori_loop(0, CHEB - 1, step, 1.0 / sigma)
        for parity in range(2):
            for vector in range(4):
                departed(coarse_copies(parity, vector))

    def prolong(parity):
        following = 1 - parity
        slots = lax.shift_right_logical(iota((128, 128), 0) & 31, 2)
        half = lax.shift_right_logical(iota((128, 128), 1), 6)
        twice = jnp.concatenate([member_t[...], member_t[...]], 1)
        for pair in (*QUADS[0], *QUADS[1]):
            high, rest = hi_lo(jnp.where(slots == 2 * pair + half, z_now[...], 0.0))
            value = dot(twice, jnp.concatenate([high, rest], 0))
            field[pair] = field[pair] + value
            wide[following, pair + 1, EDGE : EDGE + ROWS, :] = value.astype(BF)
            if pair == QUADS[0][1]:
                halo_begin(edge_halo(following))
                halo_begin(core_halo(following))
        halo_begin(middle_halo(following))

    field[...] = jnp.zeros(field.shape, F32)
    for pair in range(PAIRS):
        residual[pair] = rhs[pair]
        low[pair] = rhs[pair].astype(BF)

    def round_of(number, carry):
        parity = lax.rem(number, 2)

        @pl.when(number == 0)
        def _():
            for pair in range(PAIRS):
                load_smooth[pair].wait()
                relayout(raw_smooth, smoother, pair)

        following = 1 - parity
        more = number < 5
        chunk = stencil(parity, jnp.where(number == 3, 0.0, 1.0))
        ends = (0, 384)

        @pl.when(number > 0)
        def _():
            operator_inner(parity)
            pl.when(number == 2)(member_table)
            for pair in QUADS[1]:
                chunk(pair, 128, 256)
            halo_arrived(middle_halo(parity))
            for pair in QUADS[1]:
                for start in ends:
                    chunk(pair, start, 128)

        @pl.when(number != 2)
        def _():
            smooth_tiles(parity, 1, (0, 31))
            pl.when(more)(lambda: halo_begin(middle_halo(following)))

        @pl.when(number > 0)
        def _():
            halo_arrived(edge_halo(parity))
            for pair in QUADS[0]:
                for start in ends:
                    chunk(pair, start, 128)

        @pl.when(number != 2)
        def _():
            smooth_tiles(parity, 0, [*range(8), *range(24, 32)])
            pl.when(more)(lambda: halo_begin(edge_halo(following)))

        @pl.when(number > 0)
        def _():
            halo_arrived(core_halo(parity))
            for pair in QUADS[0]:
                chunk(pair, 128, 256)

        @pl.when(number != 2)
        def _():
            smooth_tiles(parity, 0, range(8, 24))
            pl.when(more)(lambda: halo_begin(core_halo(following)))

        @pl.when(number == 2)
        def _():
            bound_end(2)
            coarse_solve()
            prolong(parity)

        @pl.when(number == 5)
        def _():
            for pair in QUADS[0]:
                result_copy(pair).start()

        @pl.when(number != 2)
        def _():
            smooth_tiles(parity, 1, range(1, 31))

        @pl.when(number > 0)
        def _():
            for halo in (middle_halo, edge_halo, core_halo):
                halo_departed(halo(parity))

        @pl.when(number == 0)
        def _():
            coarse_bound()
            bound_begin(0)
            for pair in range(PAIRS):
                load_diag[pair].wait()
                relayout(raw_diag, diag, pair)
            bound_end(0)
            bound_begin(1)

        @pl.when(number == 1)
        def _():
            bound_end(1)
            bound_begin(2)

        return carry

    lax.fori_loop(0, 6, round_of, 0)

    for pair in QUADS[1]:
        result_copy(pair).start()
    for pair in range(PAIRS):
        result_copy(pair).wait()


def unfold(field_hbm, out_hbm, field, out, load_sem, store_sem):
    loads = [pltpu.make_async_copy(field_hbm.at[pair], field.at[pair], load_sem.at[pair]) for pair in range(PAIRS)]
    stores = [
        pltpu.make_async_copy(out.at[pl.ds(2 * pair, 2)], out_hbm.at[pl.ds(2 * pair, 2)], store_sem.at[pair])
        for pair in range(PAIRS)
    ]
    for load in loads:
        load.start()
    for pair in range(PAIRS):
        loads[pair].wait()
        for vector in range(4):
            block = field[pair, pl.ds(vector, 128, stride=4), :].T
            out[2 * pair, vector] = block[0:64]
            out[2 * pair + 1, vector] = block[64:128]
        stores[pair].start()
    for store in stores:
        store.wait()


def local(stream_total, span_total, right_side, shift_fine, diag_blocks, smoother, couplings, coefficients,
          agg_ids, coarse_columns, coarse_blocks, coarse_shift):
    columns = jnp.transpose(coarse_columns, (0, 3, 1, 2))[0]
    blocks = jnp.transpose(coarse_blocks[0, 0], (1, 0, 2))
    vm = pltpu.VMEM
    dma = pltpu.SemaphoreType.DMA
    partners = (span_total - 1) + (min(8, stream_total) - 1) + (stream_total // min(8, stream_total) - 1)
    shape = (PAIRS, ROWS, 128)
    scratch = [
        vm((8, 4, 64, 128), F32), vm((8, 64, 128), F32), vm((8, 64, 64, 128), BF), vm((8, 64, 64, 128), BF),
        vm((8, 64, 64), BF), vm((8, 8, 128), F32), vm((8, 128), jnp.int32), vm((5, 1, 32), jnp.int32),
        vm((5, 32, 4096), F32), vm((32, 64), F32),
        vm((PAIRS, 8192, 128), BF), vm((PAIRS, 8192, 128), BF), vm(shape, F32), vm(shape, F32), vm(shape, F32),
        vm(shape, F32), vm(shape, F32), vm(shape, F32), vm(shape, BF), vm((2, PAIRS + 2, WROWS, 128), BF),
        vm((8,) + shape, BF), vm((1024, 128), BF),
        vm((128, 512), BF), vm((512, 128), BF), vm((4096, 128), BF), vm((5, 32, 32), BF), vm((128, 128), F32),
        vm((128, 128), F32), vm((128, 128), F32), vm((128, 128), F32), vm((128, 128), F32),
        vm((2, 128, 128), BF), vm((2, 4, 128, 128), BF),
        vm((4, 8, 128), F32), vm((partners, 8, 128), F32), vm((128, 128), BF), vm((128, 128), BF),
        dma((16,)), dma((2, 12)), dma((2, 12)), dma((2, 4, 4)), dma((2, 4, 4)), dma((partners,)), dma((partners,)), dma((4,)),
    ]
    anywhere = pl.BlockSpec(memory_space=pl.ANY)
    result = pl.pallas_call(
        functools.partial(kernel, stream_total, span_total),
        out_shape=jax.ShapeDtypeStruct(shape, F32),
        in_specs=[anywhere] * 10,
        out_specs=anywhere,
        scratch_shapes=scratch,
        compiler_params=pltpu.CompilerParams(
            collective_id=0, has_side_effects=True, vmem_limit_bytes=60 * 1024 * 1024
        ),
        name="cycle",
    )(right_side, shift_fine, diag_blocks, smoother, couplings, coefficients, agg_ids, columns, blocks,
      coarse_shift[0, 0])
    return pl.pallas_call(
        unfold,
        out_shape=jax.ShapeDtypeStruct(right_side.shape, F32),
        in_specs=[anywhere],
        out_specs=anywhere,
        scratch_shapes=[vm(shape, F32), vm((8, 4, 64, 128), F32), dma((PAIRS,)), dma((PAIRS,))],
        compiler_params=pltpu.CompilerParams(vmem_limit_bytes=60 * 1024 * 1024),
        name="unfold",
    )(result)


def solution(mesh):
    return jax.shard_map(
        functools.partial(local, mesh.shape["stream"], mesh.shape["span"]),
        mesh=mesh,
        in_specs=(
            P("stream", None, None, "span"),
            P("stream", None, "span"),
            P("stream", None, None, "span"),
            P("stream", None, None, "span"),
            P(),
            P(None, "stream", "span"),
            P("stream", "span"),
            P("stream", "span", None, None),
            P("stream", "span", None, None, None),
            P("stream", "span", None, None),
        ),
        out_specs=P("stream", None, None, "span"),
        check_vma=False,
    )
```
